128 devices in a mesh: grp: 2 (over x_hi), tp: 8 (over y, core), sq: 8 (over x_lo, z).
Axes of the slice: x: 4 (x_hi: 2, x_lo: 2; x = x_hi * 2 + x_lo), y: 4, z: 4, core: 2. Of those that a mesh axis runs over, the one named last changes fastest.
Arguments:
- neighbour_inputs: bfloat16 [128, 128, 896], P(('grp', 'tp', 'sq')), may hold values from -6 to 6
- encoder_gain: float32 [896], replicated, may hold values from 0.5 to 1.5
- encoder_project: bfloat16 [896, 2688], replicated, may hold values from -0.1875 to 0.1875
- encoder_mix: bfloat16 [896, 896], replicated, may hold values from -0.1875 to 0.1875
- decoder_queries: bfloat16 [64, 64, 8192], P(('grp', 'sq'), None, 'tp'), may hold values from -6 to 6
- cross_pairs: bfloat16 [896, 2, 8192], P(None, None, 'tp'), may hold values from -0.1875 to 0.1875
- span_neighbours: int32 [64, 2], P(('grp', 'sq')), may hold values from 0 to 127, as said below
- grad_output: bfloat16 [64, 64, 8192], P(('grp', 'sq'), None, 'tp'), may hold values from -6 to 6
Outputs:
- cross_output: bfloat16 [64, 64, 8192], P(('grp', 'sq'), None, 'tp')
- grad_queries: bfloat16 [64, 64, 8192], P(('grp', 'sq'), None, 'tp')
- grad_cross_pairs: float32 [896, 2, 8192], P(None, None, 'tp')
- grad_encoder_project: float32 [896, 2688], P(('grp', 'tp', 'sq'))
- grad_encoder_mix: float32 [896, 896], P(('grp', 'tp', 'sq'))
- grad_neighbour_inputs: bfloat16 [128, 128, 896], P(('grp', 'tp', 'sq'))
The draws below stay inside these ranges and needn't reach their ends.
Inputs may be any that keep to these rules, and one draw needn't show every extreme that they name: `span_neighbours`: for every k, the spans k * 4 to (k + 1) * 4 - 1 together name each of the neighbours 2 * k * 4 to 2 * (k + 1) * 4 - 1 exactly once.
All inputs are finite; a program needn't handle non-finite values.
Results may differ from the reference program's by a relative error of at most 0.02.
Values may be sent and summed in bfloat16 or wider, within the bound.
No kernel may reach another device: no remote copies, remote signals or barrier semaphores. Data moves between devices by JAX's collectives and lax.ppermute only.
A program may use at most 128 MiB of HBM per device.

```python
import math
import jax
import jax.numpy as jnp
from jax import lax

D = 8192
HS = 128
ENC = 896
EHS = 128
NB_LEN = 128
CH_LEN = 64
CH_DEV = 4
SPANS = 64
NEIGH = 128


def draw_span_neighbours(key, part):
    blocks = SPANS // CH_DEV
    block_width = 2 * CH_DEV
    block_keys = jax.random.split(jax.random.fold_in(key, 17), blocks)
    orders = jax.vmap(lambda one_key: jax.random.permutation(one_key, block_width))(block_keys)
    offsets = (jnp.arange(blocks, dtype=jnp.int32) * block_width)[:, None]
    return (orders.astype(jnp.int32) + offsets).reshape(SPANS, 2)


def block_scale(rng, shape, cuts, least, high):
    gain, own = 1.0, jax.random.fold_in(rng, 6)
    for position, shards_of in cuts:
        steps = jnp.exp(jax.random.uniform(jax.random.fold_in(own, position), (shards_of,), jnp.float32, least / len(cuts), high / len(cuts)))
        gain = gain * jnp.repeat(steps, shape[position] // shards_of).reshape([-1 if axis == position else 1 for axis in range(len(shape))])
    return gain


def scatter_about(stream_key, extent, spread, most, cuts=(), held_as=jnp.bfloat16):
    values = jax.random.normal(stream_key, extent, jnp.float32) * spread
    if len(cuts) > 0:
        values = block_scale(stream_key, extent, cuts, -0.22, 0.18) * values
    return jnp.clip(values, min=-most, max=most).astype(held_as)


def setup_inputs(seed: int = 0) -> dict:
    keys = jax.random.split(jax.random.key(seed), 9)
    return {
        "neighbour_inputs": scatter_about(keys[0], (NEIGH, NB_LEN, ENC), 1.0, 6.0, ((0, 128),)),
        "encoder_gain": jnp.clip(1.0 + 0.1 * jax.random.normal(keys[1], (ENC,), jnp.float32), 0.5, 1.5),
        "encoder_project": scatter_about(keys[2], (ENC, 3 * ENC), ENC ** -0.5, 0.1875),
        "encoder_mix": scatter_about(keys[3], (ENC, ENC), ENC ** -0.5, 0.1875),
        "decoder_queries": scatter_about(keys[4], (SPANS, CH_LEN, D), 1.0, 6.0, ((0, 16), (2, 8))),
        "cross_pairs": scatter_about(keys[5], (ENC, 2, D), ENC ** -0.5, 0.1875, ((2, 8),)),
        "span_neighbours": draw_span_neighbours(jax.random.fold_in(keys[8], 71), 0),
        "grad_output": scatter_about(keys[7], (SPANS, CH_LEN, D), 1.0, 6.0, ((0, 16), (2, 8))),
    }


full_precision = lax.Precision.HIGHEST
epsilon = 1e-06

def rounded(value):
    return lax.optimization_barrier(value.astype(jnp.bfloat16)).astype(jnp.float32)

def encode(source_rows, gain_vector, project_weight, mix_weight):
    groups, length, enc_width = source_rows.shape
    heads_enc = enc_width // EHS
    variance = lax.optimization_barrier(jnp.mean(source_rows * source_rows, axis=-1, keepdims=True))
    normed = rounded(source_rows * lax.rsqrt(variance + epsilon) * gain_vector)
    projected = rounded(jnp.einsum('ntc,cf->ntf', normed, project_weight, precision=full_precision))
    projected = projected.reshape(groups, length, 3, heads_enc, EHS)
    scores = jnp.einsum('nqhd,nkhd->nhqk', projected[:, :, 0], projected[:, :, 1], precision=full_precision) / math.sqrt(EHS)
    weights = rounded(jax.nn.softmax(scores, axis=-1))
    mixed_heads = rounded(jnp.einsum('nhqk,nkhd->nqhd', weights, projected[:, :, 2], precision=full_precision))
    mixed_heads = mixed_heads.reshape(groups, length, enc_width)
    return source_rows + jnp.einsum('ntc,cf->ntf', mixed_heads, mix_weight, precision=full_precision)

def cross(sources, queries, grad_out, weight_pair):
    spans, keylen, enc_width = sources.shape
    inner_width = weight_pair.shape[1] // 2
    head_many = inner_width // HS
    score_scale = 1.0 / math.sqrt(HS)
    flat_rows = sources.reshape(spans * keylen, enc_width)
    projected = jnp.dot(flat_rows, weight_pair, preferred_element_type=jnp.float32).astype(jnp.bfloat16)
    key_rows = projected[:, :inner_width].reshape(spans, keylen, head_many, HS)
    value_rows = projected[:, inner_width:].reshape(spans, keylen, head_many, HS)
    query_rows = queries.reshape(spans, -1, head_many, HS)
    scores = jnp.einsum('cqhd,ckhd->chqk', query_rows, key_rows, preferred_element_type=jnp.float32) * score_scale
    probs_full = jax.nn.softmax(scores, axis=-1)
    probs_low = probs_full.astype(jnp.bfloat16)
    attended = jnp.einsum('chqk,ckhd->cqhd', probs_low, value_rows, preferred_element_type=jnp.float32)
    result = attended.astype(jnp.bfloat16).reshape(queries.shape)
    upstream = grad_out.reshape(query_rows.shape)
    grad_probs = jnp.einsum('cqhd,ckhd->chqk', upstream, value_rows, preferred_element_type=jnp.float32)
    grad_values = jnp.einsum('chqk,cqhd->ckhd', probs_low, upstream, preferred_element_type=jnp.float32)
    grad_scores = (probs_full * (grad_probs - lax.optimization_barrier(jnp.sum(probs_full * grad_probs, axis=-1, keepdims=True)))).astype(jnp.bfloat16)
    grad_query = (jnp.einsum('chqk,ckhd->cqhd', grad_scores, key_rows, preferred_element_type=jnp.float32) * score_scale).astype(jnp.bfloat16)
    grad_keys = jnp.einsum('chqk,cqhd->ckhd', grad_scores, query_rows, preferred_element_type=jnp.float32) * score_scale
    grad_pairs = jnp.concatenate([grad_keys.reshape(spans * keylen, inner_width), grad_values.reshape(spans * keylen, inner_width)], axis=1).astype(jnp.bfloat16)
    grad_weight = jnp.einsum('nc,nf->cf', flat_rows, grad_pairs, preferred_element_type=jnp.float32)
    grad_sources = jnp.einsum('nf,cf->nc', grad_pairs, weight_pair, preferred_element_type=jnp.float32)
    return (result, grad_query.reshape(queries.shape), grad_sources.reshape(spans, keylen, enc_width), grad_weight)

def reference(neighbour_inputs, encoder_gain, encoder_project, encoder_mix, decoder_queries, cross_pairs, span_neighbours, grad_output):
    source_rows = neighbour_inputs.astype(jnp.float32)

    def run_encoder(rows_in, project_weight, mix_weight):
        return encode(rows_in, encoder_gain, project_weight, mix_weight)
    encoded_full, pull_back = jax.vjp(run_encoder, source_rows, encoder_project.astype(jnp.float32), encoder_mix.astype(jnp.float32))
    encoded = encoded_full.astype(jnp.bfloat16)
    picked = span_neighbours.reshape(-1).astype(jnp.int32)
    keyed_rows = jnp.take(encoded, picked, axis=0).reshape(SPANS, 1, 2 * NB_LEN, ENC)
    weight_pair = cross_pairs.reshape(ENC, 2 * D)

    def visit(total, item):
        sources, queries, grad_out = item
        result, grad_query, grad_sources, grad_weight = cross(sources, queries, grad_out, weight_pair)
        return (total + grad_weight, (result, grad_query, grad_sources))
    total, (results, grad_queries, grad_sources) = lax.scan(visit, jnp.zeros((ENC, 2 * D), jnp.float32), (keyed_rows, decoder_queries.reshape(SPANS, 1, CH_LEN, D), grad_output.reshape(SPANS, 1, CH_LEN, D)))
    by_neighbour = jnp.zeros((NEIGH, NB_LEN, ENC), jnp.float32).at[picked].add(grad_sources.reshape(2 * SPANS, NB_LEN, ENC))
    grad_inputs, grad_project, grad_mix = pull_back(rounded(by_neighbour))
    return (results.reshape(SPANS, CH_LEN, D), grad_queries.reshape(SPANS, CH_LEN, D), total.reshape(ENC, 2, D), grad_project, grad_mix, grad_inputs.astype(jnp.bfloat16))
```

```python
import functools
import math

import jax
import jax.numpy as jnp
from jax import lax
from jax.experimental import pallas as pl
from jax.experimental.pallas import tpu as pltpu
from jax.sharding import Mesh
from jax.sharding import PartitionSpec as P

HS = 128
TOK = 128
ENC = 896
epsilon = 1e-06
f32 = jnp.float32
bf16 = jnp.bfloat16

FINE = ("xh", "y", "c", "xl", "z")
TP = ("y", "c")
PLANE = ("xh", "xl", "z")
LANES = 512
PARTS = 8


def turned(axis, length, by):
    pairs = [(i, (i + by) % length) for i in range(length)]
    return lambda x: lax.ppermute(x, axis, pairs)


def across(x):
    return lax.ppermute(x, "c", [(0, 1), (1, 0)])


def flipped(x):
    pairs = [(t * 8 + s, s * 8 + t) for t in range(8) for s in range(8)]
    return lax.ppermute(x, ("y", "c", "xl", "z"), pairs)


def dot(a, b, contract):
    return lax.dot_general(a, b, ((contract[:1], contract[1:]), ((), ())), preferred_element_type=f32)


def nn(a, b):
    return dot(a, b, (1, 0))


def nt(a, b):
    return dot(a, b, (1, 1))


def tn(a, b):
    return dot(a, b, (0, 0))


def params(mib, n=0):
    more = {"dimension_semantics": ("arbitrary",) * n} if n else {}
    return pltpu.CompilerParams(vmem_limit_bytes=mib * 2**20, **more)


def cost(flops, size):
    return pl.CostEstimate(flops=flops, bytes_accessed=size, transcendentals=0)


def softmax(scores):
    e = jnp.exp(scores - jnp.max(scores, axis=-1, keepdims=True))
    return e / jnp.sum(e, axis=-1, keepdims=True)


def head(ref, h, block=0):
    start = block * ENC + h * HS
    return ref[:, start : start + HS]


def encode_kernel(x_ref, gain_ref, project_ref, mix_ref, encoded_ref, normed_ref, projected_ref, mixed_ref):
    x = x_ref[...].astype(f32)
    r = lax.rsqrt(jnp.mean(x * x, axis=-1, keepdims=True) + epsilon)
    normed_ref[...] = (x * r * gain_ref[...]).astype(bf16)
    projected_ref[...] = nn(normed_ref[...], project_ref[...]).astype(bf16)
    for h in range(ENC // HS):
        q, k, v = (head(projected_ref, h, b) for b in range(3))
        w = softmax(nt(q, k) / math.sqrt(HS)).astype(bf16)
        mixed_ref[:, h * HS : (h + 1) * HS] = nn(w, v).astype(bf16)
    encoded_ref[...] = (x + nn(mixed_ref[...], mix_ref[...])).astype(bf16)


def encode(x, gain, project, mix):
    shape = jax.ShapeDtypeStruct((TOK, ENC), bf16)
    wide = jax.ShapeDtypeStruct((TOK, 3 * ENC), bf16)
    return pl.pallas_call(
        encode_kernel,
        out_shape=(shape, shape, wide, shape),
        compiler_params=params(24),
        cost_estimate=cost(10**9, 8 * 10**6),
    )(x, gain, project, mix)


def spread_kernel(normed_ref, mixed_ref, out_ref):
    column = lax.broadcasted_iota(jnp.int32, (ENC, 1024), 1)
    row = lax.broadcasted_iota(jnp.int32, (ENC, 1024), 0)
    place = jnp.where((column % 8 < 7) & (row == column // 8 * 7 + column % 8), 1.0, 0.0).astype(bf16)
    out_ref[:, :1024] = nn(normed_ref[...], place).astype(bf16)
    out_ref[:, 1024:] = nn(mixed_ref[...], place).astype(bf16)


def spread(normed, mixed):
    return pl.pallas_call(
        spread_kernel,
        out_shape=jax.ShapeDtypeStruct((TOK, 2048), bf16),
        compiler_params=params(24),
        cost_estimate=cost(5 * 10**8, 10**6),
    )(normed, mixed)


def pairs_kernel(first_ref, second_ref, weight_ref, *rest):
    held_ref, out_ref = rest[-2:]
    held_ref[0, 0] = first_ref[...]
    held_ref[1, 0] = second_ref[...]
    out_ref[0, 0] = nn(first_ref[...], weight_ref[...]).astype(bf16)
    out_ref[1, 0] = nn(second_ref[...], weight_ref[...]).astype(bf16)


def pairs_of(step, first, second, weight, before):
    many = 4
    width = weight.shape[1] // many
    kept = [pl.BlockSpec(memory_space=pl.ANY)] * len(before)
    return pl.pallas_call(
        pairs_kernel,
        grid=(many,),
        in_specs=[
            pl.BlockSpec((TOK, ENC), lambda i: (0, 0)),
            pl.BlockSpec((TOK, ENC), lambda i: (0, 0)),
            pl.BlockSpec((ENC, width), lambda i: (0, i)),
            *kept,
        ],
        out_specs=(
            pl.BlockSpec((2, 1, TOK, ENC), lambda i: (0, step, 0, 0)),
            pl.BlockSpec((2, 1, TOK, width), lambda i: (0, step, 0, i)),
        ),
        out_shape=(
            jax.ShapeDtypeStruct((2, 4, TOK, ENC), bf16),
            jax.ShapeDtypeStruct((2, 4, TOK, weight.shape[1]), bf16),
        ),
        input_output_aliases={3: 0, 4: 1} if before else {},
        compiler_params=params(16, 1),
        cost_estimate=cost(10**9, 6 * 10**6),
    )(first, second, weight, *before)


def cross_kernel(slots_ref, q_ref, up_ref, one_ref, two_ref, out_ref, grad_ref, pairs_ref):
    span = pl.program_id(0)
    slots = (slots_ref[2 * span], slots_ref[2 * span + 1])
    inner = q_ref.shape[2]
    scale = 1.0 / math.sqrt(HS)
    for h in range(inner // HS):
        at = slice(h * HS, (h + 1) * HS)
        up = slice(inner + h * HS, inner + (h + 1) * HS)
        q = q_ref[0, :, at]
        g = up_ref[0, :, at]
        k = jnp.concatenate([one_ref[0, :, at], two_ref[0, :, at]], axis=0)
        v = jnp.concatenate([one_ref[0, :, up], two_ref[0, :, up]], axis=0)
        probs = softmax(nt(q, k) * scale)
        low = probs.astype(bf16)
        out_ref[0, :, at] = nn(low, v).astype(bf16)
        grad_probs = nt(g, v)
        grad_values = tn(low, g).astype(bf16)
        total = jnp.sum(probs * grad_probs, axis=-1, keepdims=True)
        grad_scores = (probs * (grad_probs - total)).astype(bf16)
        grad_ref[0, :, at] = (nn(grad_scores, k) * scale).astype(bf16)
        grad_keys = (tn(grad_scores, q) * scale).astype(bf16)
        for n in range(2):
            pairs_ref[slots[n], :, at] = grad_keys[n * TOK : (n + 1) * TOK]
            pairs_ref[slots[n], :, up] = grad_values[n * TOK : (n + 1) * TOK]


def cross(slots, queries, upstream, pairs):
    spans, length, inner = queries.shape
    whole = pl.BlockSpec((1, length, inner), lambda i, s: (i, 0, 0))
    return pl.pallas_call(
        cross_kernel,
        grid_spec=pltpu.PrefetchScalarGridSpec(
            num_scalar_prefetch=1,
            grid=(spans,),
            in_specs=[
                whole,
                whole,
                pl.BlockSpec((1, TOK, 2 * inner), lambda i, s: (s[2 * i], 0, 0)),
                pl.BlockSpec((1, TOK, 2 * inner), lambda i, s: (s[2 * i + 1], 0, 0)),
            ],
            out_specs=(
                whole,
                whole,
                pl.BlockSpec((2 * spans, TOK, 2 * inner), lambda i, s: (0, 0, 0)),
            ),
        ),
        out_shape=(
            jax.ShapeDtypeStruct(queries.shape, bf16),
            jax.ShapeDtypeStruct(queries.shape, bf16),
            jax.ShapeDtypeStruct((2 * spans, TOK, 2 * inner), bf16),
        ),
        compiler_params=params(32, 1),
        cost_estimate=cost(3 * 10**9, 12 * 10**6),
    )(slots, queries, upstream, pairs, pairs)


def columns_of(at):
    return at // LANES, slice(at % LANES, at % LANES + HS)


def backward_kernel(grad_ref, projected_ref, mix_ref, out_ref):
    grad = grad_ref[...]
    grad_mixed = nt(grad, mix_ref[...]).astype(bf16)
    heads = ENC // HS
    for j in range(PARTS * LANES // HS):
        part, lanes = columns_of(j * HS)
        if j < 3 * heads:
            continue
        near = j - 24
        if 0 <= near < heads:
            out_ref[part, :, lanes] = grad[:, near * HS : (near + 1) * HS]
        else:
            out_ref[part, :, lanes] = jnp.zeros((TOK, HS), bf16)
    for h in range(heads):
        q, k, v = (head(projected_ref, h, b) for b in range(3))
        g = grad_mixed[:, h * HS : (h + 1) * HS]
        probs = softmax(nt(q, k) / math.sqrt(HS))
        grad_probs = nt(g, v).astype(bf16).astype(f32)
        total = jnp.sum(probs * grad_probs, axis=-1, keepdims=True)
        grad_scores = (probs * (grad_probs - total) / math.sqrt(HS)).astype(bf16)
        for b, value in enumerate(
            (nn(grad_scores, k), tn(grad_scores, q), tn(probs.astype(bf16), g))
        ):
            part, lanes = columns_of(b * ENC + h * HS)
            out_ref[part, :, lanes] = value.astype(bf16)


def backward(grad, projected, mix):
    return pl.pallas_call(
        backward_kernel,
        out_shape=jax.ShapeDtypeStruct((PARTS, TOK, LANES), bf16),
        compiler_params=params(24),
        cost_estimate=cost(6 * 10**8, 4 * 10**6),
    )(grad, projected, mix)


def inputs_kernel(x_ref, gain_ref, project_ref, parts_ref, grad_ref, out_ref):
    many = 3 * ENC // LANES
    total = nt(parts_ref[0], project_ref[:, :LANES])
    for j in range(1, many):
        total += nt(parts_ref[j], project_ref[:, j * LANES : (j + 1) * LANES])
    rest = 3 * ENC - many * LANES
    total += nt(parts_ref[many][:, :rest], project_ref[:, many * LANES :])
    u = total.astype(bf16).astype(f32) * gain_ref[...]
    x = x_ref[...].astype(f32)
    r = lax.rsqrt(jnp.mean(x * x, axis=-1, keepdims=True) + epsilon)
    slope = jnp.mean(x * u, axis=-1, keepdims=True) * (r * r * r)
    out_ref[...] = (r * u - x * slope + grad_ref[...].astype(f32)).astype(bf16)


def inputs_grad(x, gain, project, parts, grad):
    return pl.pallas_call(
        inputs_kernel,
        out_shape=jax.ShapeDtypeStruct((TOK, ENC), bf16),
        compiler_params=params(24),
        cost_estimate=cost(6 * 10**8, 6 * 10**6),
    )(x, gain, project, parts, grad)


def shards(
    neighbour_inputs,
    encoder_gain,
    encoder_project,
    encoder_mix,
    decoder_queries,
    cross_pairs,
    span_neighbours,
    grad_output,
):
    gain = encoder_gain.reshape(1, ENC)
    y, core = lax.axis_index("y"), lax.axis_index("c")
    inner = cross_pairs.shape[2]
    x = flipped(neighbour_inputs[0])
    weight = lax.optimization_barrier(cross_pairs.reshape(ENC, 2 * inner))
    encoded, normed, projected, mixed = encode(x, gain, encoder_project, encoder_mix)

    before = ()
    for step in range(4):
        first = encoded if step == 0 else turned("y", 4, -step)(encoded)
        before = pairs_of(step, first, across(first), weight, before)
    sources, pairs = before
    operands = lax.all_gather(spread(normed, mixed), TP, tiled=True)

    named = span_neighbours.reshape(-1) % 8
    slots = (named % 2 != core) * 4 + (named // 2 - y) % 4
    result, grad_queries, grad_pairs = cross(
        slots.astype(jnp.int32), decoder_queries, grad_output, pairs.reshape(8, TOK, 2 * inner)
    )

    far = nt(grad_pairs[4:].reshape(4 * TOK, 2 * inner), weight).astype(bf16)
    brought = across(far)
    near = nt(grad_pairs[:4].reshape(4 * TOK, 2 * inner), weight)
    grad_weight = tn(sources.reshape(8 * TOK, ENC), grad_pairs.reshape(8 * TOK, 2 * inner)).astype(bf16)
    summed = (near + brought.astype(f32)).reshape(4, TOK, ENC)
    total = summed[0]
    for step in range(1, 4):
        total += turned("y", 4, step)(summed[step].astype(bf16)).astype(f32)
    grad_encoded = total.astype(bf16)

    grad_cross = lax.psum(grad_weight, PLANE)
    grad_cross = grad_cross.astype(f32).reshape(cross_pairs.shape)

    parts = backward(grad_encoded, projected, encoder_mix)
    all_parts = lax.all_to_all(parts, TP, 0, 0, tiled=True).reshape(8 * TOK, LANES)
    mine = jnp.where(y * 2 + core < 6, operands[:, :1024], operands[:, 1024:])
    encoder_grad = tn(mine, all_parts).astype(bf16).reshape(128, 8, LANES)
    arrived = lax.all_to_all(encoder_grad, FINE, 0, 0, tiled=True).astype(f32)
    arrived = arrived.reshape(2, 8, 8, 8, LANES).sum(axis=(0, 2))
    rows = jnp.swapaxes(arrived, 0, 1).reshape(8, 8 * LANES)[:7]
    grad_inputs = flipped(inputs_grad(x, gain, encoder_project, parts, grad_encoded))
    return (
        result,
        grad_queries,
        grad_cross,
        rows[:, : 3 * ENC],
        rows[:, 6 * LANES : 6 * LANES + ENC],
        grad_inputs[None],
    )


def solution(mesh):
    fine = Mesh(mesh.devices.reshape(2, 4, 2, 2, 4), FINE)
    heads = P(PLANE, None, TP)
    placed = (
        P(FINE, None, None),
        P(),
        P(),
        P(),
        heads,
        P(None, None, TP),
        P(PLANE, None),
        heads,
    )
    return jax.shard_map(
        shards,
        mesh=fine,
        in_specs=placed,
        out_specs=(
            heads,
            heads,
            P(None, None, TP),
            P(FINE, None),
            P(FINE, None),
            P(FINE, None, None),
        ),
        check_vma=False,
    )
```

```python
import functools
import math

import jax
import jax.numpy as jnp
from jax import lax
from jax.experimental import pallas as pl
from jax.experimental.pallas import tpu as pltpu
from jax.sharding import Mesh
from jax.sharding import PartitionSpec as P

HS = 128
TOK = 128
ENC = 896
epsilon = 1e-06
f32 = jnp.float32
bf16 = jnp.bfloat16

FINE = ("xh", "y", "c", "xl", "z")
TP = ("y", "c")
PLANE = ("xh", "xl", "z")
LANES = 512
PARTS = 8


def turned(axis, length, by):
    pairs = [(i, (i + by) % length) for i in range(length)]
    return lambda x: lax.ppermute(x, axis, pairs)


def across(x):
    return lax.ppermute(x, "c", [(0, 1), (1, 0)])


def flipped(x):
    pairs = [(t * 8 + s, s * 8 + t) for t in range(8) for s in range(8)]
    return lax.ppermute(x, ("y", "c", "xl", "z"), pairs)


def dot(a, b, contract):
    return lax.dot_general(a, b, ((contract[:1], contract[1:]), ((), ())), preferred_element_type=f32)


def nn(a, b):
    return dot(a, b, (1, 0))


def nt(a, b):
    return dot(a, b, (1, 1))


def tn(a, b):
    return dot(a, b, (0, 0))


def params(mib, n=0):
    more = {"dimension_semantics": ("arbitrary",) * n} if n else {}
    return pltpu.CompilerParams(vmem_limit_bytes=mib * 2**20, **more)


def cost(flops, size):
    return pl.CostEstimate(flops=flops, bytes_accessed=size, transcendentals=0)


def softmax(scores):
    e = jnp.exp(scores - jnp.max(scores, axis=-1, keepdims=True))
    return e / jnp.sum(e, axis=-1, keepdims=True)


def head(ref, h, block=0):
    start = block * ENC + h * HS
    return ref[:, start : start + HS]


def encode_kernel(x_ref, gain_ref, project_ref, mix_ref, encoded_ref, normed_ref, projected_ref, mixed_ref):
    x = x_ref[...].astype(f32)
    r = lax.rsqrt(jnp.mean(x * x, axis=-1, keepdims=True) + epsilon)
    normed_ref[...] = (x * r * gain_ref[...]).astype(bf16)
    projected_ref[...] = nn(normed_ref[...], project_ref[...]).astype(bf16)
    for h in range(ENC // HS):
        q, k, v = (head(projected_ref, h, b) for b in range(3))
        w = softmax(nt(q, k) / math.sqrt(HS)).astype(bf16)
        mixed_ref[:, h * HS : (h + 1) * HS] = nn(w, v).astype(bf16)
    encoded_ref[...] = (x + nn(mixed_ref[...], mix_ref[...])).astype(bf16)


def encode(x, gain, project, mix):
    shape = jax.ShapeDtypeStruct((TOK, ENC), bf16)
    wide = jax.ShapeDtypeStruct((TOK, 3 * ENC), bf16)
    return pl.pallas_call(
        encode_kernel,
        out_shape=(shape, shape, wide, shape),
        compiler_params=params(24),
        cost_estimate=cost(10**9, 8 * 10**6),
    )(x, gain, project, mix)


def spread_kernel(normed_ref, mixed_ref, out_ref):
    column = lax.broadcasted_iota(jnp.int32, (ENC, 1024), 1)
    row = lax.broadcasted_iota(jnp.int32, (ENC, 1024), 0)
    place = jnp.where((column % 8 < 7) & (row == column // 8 * 7 + column % 8), 1.0, 0.0).astype(bf16)
    out_ref[:, :1024] = nn(normed_ref[...], place).astype(bf16)
    out_ref[:, 1024:] = nn(mixed_ref[...], place).astype(bf16)


def spread(normed, mixed):
    return pl.pallas_call(
        spread_kernel,
        out_shape=jax.ShapeDtypeStruct((TOK, 2048), bf16),
        compiler_params=params(24),
        cost_estimate=cost(5 * 10**8, 10**6),
    )(normed, mixed)


def cross_kernel(slots_ref, q_ref, up_ref, weight_ref, *rest):
    sources, (out_ref, grad_ref, pairs_ref, rows_ref, held_ref) = rest[:8], rest[8:]

    @pl.when(pl.program_id(0) == 0)
    def _():
        for n, source in enumerate(sources):
            rows_ref[n * TOK : (n + 1) * TOK] = source[...]

    held_ref[...] = nn(rows_ref[...], weight_ref[...]).astype(bf16)
    scale = 1.0 / math.sqrt(HS)
    spans = range(q_ref.shape[0])
    rows = [
        [pl.ds(pl.multiple_of(slots_ref[2 * c + n] * TOK, TOK), TOK) for n in range(2)]
        for c in spans
    ]
    k = [jnp.concatenate([held_ref[r, :HS] for r in rows[c]], axis=0) for c in spans]
    v = [jnp.concatenate([held_ref[r, HS:] for r in rows[c]], axis=0) for c in spans]
    scores = [nt(q_ref[c], k[c]) * scale for c in spans]
    grad_probs = [nt(up_ref[c], v[c]) for c in spans]
    probs = [softmax(scores[c]) for c in spans]
    low = [probs[c].astype(bf16) for c in spans]
    totals = [jnp.sum(probs[c] * grad_probs[c], axis=-1, keepdims=True) for c in spans]
    grad_scores = [(probs[c] * (grad_probs[c] - totals[c])).astype(bf16) for c in spans]
    for c in spans:
        out_ref[c] = nn(low[c], v[c]).astype(bf16)
        grad_ref[c] = (nn(grad_scores[c], k[c]) * scale).astype(bf16)
    for c in spans:
        grad_keys = (tn(grad_scores[c], q_ref[c]) * scale).astype(bf16)
        grad_values = tn(low[c], up_ref[c]).astype(bf16)
        for n in range(2):
            pairs_ref[rows[c][n], :HS] = grad_keys[n * TOK : (n + 1) * TOK]
            pairs_ref[rows[c][n], HS:] = grad_values[n * TOK : (n + 1) * TOK]


def cross(slots, queries, upstream, weight, sources):
    spans, length, inner = queries.shape
    rows = len(sources) * TOK
    column = pl.BlockSpec((spans, length, HS), lambda i, s: (0, 0, i))
    return pl.pallas_call(
        cross_kernel,
        grid_spec=pltpu.PrefetchScalarGridSpec(
            num_scalar_prefetch=1,
            grid=(inner // HS,),
            in_specs=[
                column,
                column,
                pl.BlockSpec((ENC, 2 * HS), lambda i, s: (0, i)),
                *[pl.BlockSpec((TOK, ENC), lambda i, s: (0, 0))] * len(sources),
            ],
            out_specs=(column, column, pl.BlockSpec((rows, 2 * HS), lambda i, s: (0, i))),
            scratch_shapes=[pltpu.VMEM((rows, ENC), bf16), pltpu.VMEM((rows, 2 * HS), bf16)],
        ),
        out_shape=(
            jax.ShapeDtypeStruct(queries.shape, bf16),
            jax.ShapeDtypeStruct(queries.shape, bf16),
            jax.ShapeDtypeStruct((rows, 2 * inner), bf16),
        ),
        compiler_params=params(24, 1),
        cost_estimate=cost(12 * 10**9, 12 * 10**6),
    )(slots, queries, upstream, weight, *sources)


def weight_kernel(order_ref, pairs_ref, *rest):
    sources, outs, turned_ref = rest[:8], rest[8:-1], rest[-1]
    for n, source in enumerate(sources):
        turned_ref[:, n * TOK : (n + 1) * TOK] = source[...].T
    for i, out in enumerate(outs):
        at = pl.ds(pl.multiple_of(order_ref[i] * 2 * HS, 2 * HS), 2 * HS)
        out[...] = nn(turned_ref[...], pairs_ref[:, at]).astype(bf16)


def weight_blocks(order, pairs, sources):
    heads = pairs.shape[1] // (2 * HS)
    vmem = pl.BlockSpec(memory_space=pltpu.VMEM)
    return pl.pallas_call(
        weight_kernel,
        in_specs=[pl.BlockSpec(memory_space=pltpu.SMEM)] + [vmem] * (1 + len(sources)),
        out_specs=(vmem,) * heads,
        out_shape=(jax.ShapeDtypeStruct((ENC, 2 * HS), bf16),) * heads,
        scratch_shapes=[pltpu.VMEM((ENC, len(sources) * TOK), bf16)],
        compiler_params=params(24),
        cost_estimate=cost(4 * 10**9, 10**7),
    )(order, pairs, *sources)


def plane_sum(blocks, first, second, at_second):
    total = blocks[0].astype(f32)
    for d in range(1, 4):
        total += turned(first, 4, d)(blocks[d]).astype(f32)
    total = total.astype(bf16)
    size = total.shape[0] // 4
    cuts = [lax.dynamic_slice_in_dim(total, (at_second + d) % 4 * size, size) for d in range(4)]
    piece = cuts[0].astype(f32)
    for d in range(1, 4):
        piece += turned(second, 4, d)(cuts[d]).astype(f32)
    piece = piece.astype(bf16)
    line = jnp.stack([piece] + [turned(second, 4, -d)(piece) for d in range(1, 4)])
    return [line] + [turned(first, 4, -d)(line) for d in range(1, 4)]


def place_kernel(at_ref, *rest):
    lines, out_ref = rest[:8], rest[8]
    size = lines[0].shape[1]
    for half in range(2):
        for h in range(4):
            for d in range(4):

                @pl.when((at_ref[half] + d) % 4 == h)
                def _():
                    for b in range(2):
                        value = lines[4 * half + d][0, :, b * HS : (b + 1) * HS]
                        start = (half * 4 + h) * 2 + b
                        out_ref[pl.ds(start, size, stride=16), :] = value.astype(f32)


def placed_blocks(at, lines):
    size = lines[0].shape[1]
    return pl.pallas_call(
        place_kernel,
        grid_spec=pltpu.PrefetchScalarGridSpec(
            num_scalar_prefetch=1,
            grid=(4,),
            in_specs=[
                pl.BlockSpec((1, size, 2 * HS), lambda i, s, o=1 - n // 4: ((i - s[o] + 4) % 4, 0, 0))
                for n in range(8)
            ],
            out_specs=pl.BlockSpec((size * 16, HS), lambda i, s: (i, 0)),
        ),
        out_shape=jax.ShapeDtypeStruct((4 * size * 16, HS), f32),
        compiler_params=params(16, 1),
        cost_estimate=cost(10**6, 11 * 10**6),
    )(at, *lines)


def columns_of(at):
    return at // LANES, slice(at % LANES, at % LANES + HS)


def backward_kernel(grad_ref, projected_ref, mix_ref, out_ref):
    grad = grad_ref[...]
    grad_mixed = nt(grad, mix_ref[...]).astype(bf16)
    heads = ENC // HS
    for j in range(PARTS * LANES // HS):
        part, lanes = columns_of(j * HS)
        if j < 3 * heads:
            continue
        near = j - 24
        if 0 <= near < heads:
            out_ref[part, :, lanes] = grad[:, near * HS : (near + 1) * HS]
        else:
            out_ref[part, :, lanes] = jnp.zeros((TOK, HS), bf16)
    for h in range(heads):
        q, k, v = (head(projected_ref, h, b) for b in range(3))
        g = grad_mixed[:, h * HS : (h + 1) * HS]
        probs = softmax(nt(q, k) / math.sqrt(HS))
        grad_probs = nt(g, v).astype(bf16).astype(f32)
        total = jnp.sum(probs * grad_probs, axis=-1, keepdims=True)
        grad_scores = (probs * (grad_probs - total) / math.sqrt(HS)).astype(bf16)
        for b, value in enumerate(
            (nn(grad_scores, k), tn(grad_scores, q), tn(probs.astype(bf16), g))
        ):
            part, lanes = columns_of(b * ENC + h * HS)
            out_ref[part, :, lanes] = value.astype(bf16)


def backward(grad, projected, mix):
    return pl.pallas_call(
        backward_kernel,
        out_shape=jax.ShapeDtypeStruct((PARTS, TOK, LANES), bf16),
        compiler_params=params(24),
        cost_estimate=cost(6 * 10**8, 4 * 10**6),
    )(grad, projected, mix)


def inputs_kernel(x_ref, gain_ref, project_ref, parts_ref, grad_ref, out_ref):
    many = 3 * ENC // LANES
    total = nt(parts_ref[0], project_ref[:, :LANES])
    for j in range(1, many):
        total += nt(parts_ref[j], project_ref[:, j * LANES : (j + 1) * LANES])
    rest = 3 * ENC - many * LANES
    total += nt(parts_ref[many][:, :rest], project_ref[:, many * LANES :])
    u = total.astype(bf16).astype(f32) * gain_ref[...]
    x = x_ref[...].astype(f32)
    r = lax.rsqrt(jnp.mean(x * x, axis=-1, keepdims=True) + epsilon)
    slope = jnp.mean(x * u, axis=-1, keepdims=True) * (r * r * r)
    out_ref[...] = (r * u - x * slope + grad_ref[...].astype(f32)).astype(bf16)


def inputs_grad(x, gain, project, parts, grad):
    return pl.pallas_call(
        inputs_kernel,
        out_shape=jax.ShapeDtypeStruct((TOK, ENC), bf16),
        compiler_params=params(24),
        cost_estimate=cost(6 * 10**8, 6 * 10**6),
    )(x, gain, project, parts, grad)


def shards(
    neighbour_inputs,
    encoder_gain,
    encoder_project,
    encoder_mix,
    decoder_queries,
    cross_pairs,
    span_neighbours,
    grad_output,
):
    gain = encoder_gain.reshape(1, ENC)
    y, core = lax.axis_index("y"), lax.axis_index("c")
    inner = cross_pairs.shape[2]
    x = flipped(neighbour_inputs[0])
    heads = inner // HS
    weight = cross_pairs.reshape(ENC, 2, heads, HS).swapaxes(1, 2).reshape(ENC, 2 * inner)
    weight = lax.optimization_barrier(weight)
    encoded, normed, projected, mixed = encode(x, gain, encoder_project, encoder_mix)

    column = [encoded] + [turned("y", 4, -step)(encoded) for step in range(1, 4)]
    sources = column + [across(one) for one in column]
    normed, mixed, _ = lax.optimization_barrier((normed, mixed, sources[6]))
    operands = lax.all_gather(spread(normed, mixed), TP, tiled=True)

    named = span_neighbours.reshape(-1) % 8
    slots = (named % 2 != core) * 4 + (named // 2 - y) % 4
    result, grad_queries, grad_pairs = cross(
        slots.astype(jnp.int32), decoder_queries, grad_output, weight, sources
    )

    far = nt(grad_pairs[4 * TOK :], weight).astype(bf16)
    brought = across(far)
    near = nt(grad_pairs[: 4 * TOK], weight)

    at_x = lax.axis_index("xh") * 2 + lax.axis_index("xl")
    at_z = lax.axis_index("z")
    steps = jnp.arange(4, dtype=jnp.int32)
    order = jnp.concatenate([(at_x + steps) % 4, 4 + (at_z + steps) % 4])
    blocks = weight_blocks(order, grad_pairs, sources)
    lines = plane_sum(blocks[:4], ("xh", "xl"), "z", at_z) + plane_sum(
        blocks[4:], "z", ("xh", "xl"), at_x
    )
    grad_cross = placed_blocks(jnp.stack([at_x, at_z]).astype(jnp.int32), lines)
    grad_cross = grad_cross.reshape(ENC, heads, 2, HS).swapaxes(1, 2).reshape(cross_pairs.shape)

    summed = (near + brought.astype(f32)).reshape(4, TOK, ENC)
    total = summed[0]
    for step in range(1, 4):
        total += turned("y", 4, step)(summed[step].astype(bf16)).astype(f32)
    grad_encoded = total.astype(bf16)

    parts = backward(grad_encoded, projected, encoder_mix)
    all_parts = lax.all_to_all(parts, TP, 0, 0, tiled=True).reshape(8 * TOK, LANES)
    mine = jnp.where(y * 2 + core < 6, operands[:, :1024], operands[:, 1024:])
    encoder_grad = tn(mine, all_parts).astype(bf16).reshape(128, 8, LANES)
    arrived = lax.all_to_all(encoder_grad, FINE, 0, 0, tiled=True).astype(f32)
    arrived = arrived.reshape(2, 8, 8, 8, LANES).sum(axis=(0, 2))
    rows = jnp.swapaxes(arrived, 0, 1).reshape(8, 8 * LANES)[:7]
    grad_inputs = flipped(inputs_grad(x, gain, encoder_project, parts, grad_encoded))
    return (
        result,
        grad_queries,
        grad_cross,
        rows[:, : 3 * ENC],
        rows[:, 6 * LANES : 6 * LANES + ENC],
        grad_inputs[None],
    )


def solution(mesh):
    fine = Mesh(mesh.devices.reshape(2, 4, 2, 2, 4), FINE)
    heads = P(PLANE, None, TP)
    placed = (
        P(FINE, None, None),
        P(),
        P(),
        P(),
        heads,
        P(None, None, TP),
        P(PLANE, None),
        heads,
    )
    return jax.shard_map(
        shards,
        mesh=fine,
        in_specs=placed,
        out_specs=(
            heads,
            heads,
            P(None, None, TP),
            P(FINE, None),
            P(FINE, None),
            P(FINE, None, None),
        ),
        check_vma=False,
    )
```

```python
import functools
import math

import jax
import jax.numpy as jnp
from jax import lax
from jax.experimental import pallas as pl
from jax.experimental.pallas import tpu as pltpu
from jax.sharding import Mesh
from jax.sharding import PartitionSpec as P

HS = 128
TOK = 128
ENC = 896
epsilon = 1e-06
f32 = jnp.float32
bf16 = jnp.bfloat16

FINE = ("xh", "y", "c", "xl", "z")
TP = ("y", "c")
PLANE = ("xh", "xl", "z")
LANES = 512
PARTS = 8


def turned(axis, length, by):
    pairs = [(i, (i + by) % length) for i in range(length)]
    return lambda x: lax.ppermute(x, axis, pairs)


def across(x):
    return lax.ppermute(x, "c", [(0, 1), (1, 0)])


def flipped(x):
    pairs = [(t * 8 + s, s * 8 + t) for t in range(8) for s in range(8)]
    return lax.ppermute(x, ("y", "c", "xl", "z"), pairs)


def dot(a, b, contract):
    return lax.dot_general(a, b, ((contract[:1], contract[1:]), ((), ())), preferred_element_type=f32)


def nn(a, b):
    return dot(a, b, (1, 0))


def nt(a, b):
    return dot(a, b, (1, 1))


def tn(a, b):
    return dot(a, b, (0, 0))


def params(mib, n=0):
    more = {"dimension_semantics": ("arbitrary",) * n} if n else {}
    return pltpu.CompilerParams(vmem_limit_bytes=mib * 2**20, **more)


def cost(flops, size):
    return pl.CostEstimate(flops=flops, bytes_accessed=size, transcendentals=0)


def softmax(scores):
    e = jnp.exp(scores - jnp.max(scores, axis=-1, keepdims=True))
    return e / jnp.sum(e, axis=-1, keepdims=True)


def head(ref, h, block=0):
    start = block * ENC + h * HS
    return ref[:, start : start + HS]


def encode_kernel(
    x_ref, gain_ref, project_ref, mix_ref, encoded_ref, normed_ref, projected_ref, mixed_ref, project, mix, sems
):
    thirds = [slice(b * ENC, (b + 1) * ENC) for b in range(3)]
    copies = [
        pltpu.make_async_copy(project_ref.at[:, at], project.at[:, at], sems.at[b])
        for b, at in enumerate(thirds)
    ]
    copies.append(pltpu.make_async_copy(mix_ref, mix, sems.at[3]))
    for copy in copies:
        copy.start()
    x = x_ref[...].astype(f32)
    r = lax.rsqrt(jnp.mean(x * x, axis=-1, keepdims=True) + epsilon)
    normed_ref[...] = (x * r * gain_ref[...]).astype(bf16)
    for b, at in enumerate(thirds):
        copies[b].wait()
        projected_ref[:, at] = nn(normed_ref[...], project[:, at]).astype(bf16)
    heads = range(ENC // HS)
    scores = [nt(head(projected_ref, h, 0), head(projected_ref, h, 1)) / math.sqrt(HS) for h in heads]
    weights = [softmax(s).astype(bf16) for s in scores]
    for h in heads:
        mixed_ref[:, h * HS : (h + 1) * HS] = nn(weights[h], head(projected_ref, h, 2)).astype(bf16)
    copies[3].wait()
    encoded_ref[...] = (x + nn(mixed_ref[...], mix[...])).astype(bf16)


def encode(x, gain, project, mix):
    shape = jax.ShapeDtypeStruct((TOK, ENC), bf16)
    wide = jax.ShapeDtypeStruct((TOK, 3 * ENC), bf16)
    vmem = pl.BlockSpec(memory_space=pltpu.VMEM)
    far = pl.BlockSpec(memory_space=pl.ANY)
    return pl.pallas_call(
        encode_kernel,
        in_specs=[vmem, vmem, far, far],
        out_specs=[vmem] * 4,
        out_shape=[shape, shape, wide, shape],
        scratch_shapes=[
            pltpu.VMEM((ENC, 3 * ENC), bf16),
            pltpu.VMEM((ENC, ENC), bf16),
            pltpu.SemaphoreType.DMA((4,)),
        ],
        compiler_params=params(58),
        cost_estimate=cost(10**9, 8 * 10**6),
    )(x, gain, project, mix)


def spread_kernel(normed_ref, mixed_ref, out_ref):
    column = lax.broadcasted_iota(jnp.int32, (ENC, 1024), 1)
    row = lax.broadcasted_iota(jnp.int32, (ENC, 1024), 0)
    place = jnp.where((column % 8 < 7) & (row == column // 8 * 7 + column % 8), 1.0, 0.0).astype(bf16)
    out_ref[:, :1024] = nn(normed_ref[...], place).astype(bf16)
    out_ref[:, 1024:] = nn(mixed_ref[...], place).astype(bf16)


def spread(normed, mixed):
    return pl.pallas_call(
        spread_kernel,
        out_shape=jax.ShapeDtypeStruct((TOK, 2048), bf16),
        compiler_params=params(24),
        cost_estimate=cost(5 * 10**8, 10**6),
    )(normed, mixed)


def cross_kernel(per, slots_ref, q_ref, up_ref, weight_ref, *rest):
    sources, (out_ref, grad_ref, pairs_ref, sum_ref, rows_ref, turned_ref, held_ref) = rest[:8], rest[8:]

    @pl.when(pl.program_id(0) == 0)
    def _():
        for n, source in enumerate(sources):
            rows_ref[n * TOK : (n + 1) * TOK] = source[...]
            turned_ref[:, n * TOK : (n + 1) * TOK] = source[...].T

    scale = 1.0 / math.sqrt(HS)
    length = q_ref.shape[1]
    none = jnp.zeros((length, HS), bf16)
    spans = range(q_ref.shape[0])
    rows = [
        [pl.ds(pl.multiple_of(slots_ref[2 * c + n] * TOK, TOK), TOK) for n in range(2)] for c in spans
    ]
    held_ref[...] = nn(rows_ref[...], weight_ref[...]).astype(bf16)
    for first in range(0, per, 2):
        units = []
        for h in range(first, first + 2):
            at, pair = slice(h * HS, (h + 1) * HS), slice(2 * h * HS, 2 * (h + 1) * HS)
            for c in spans:
                held = jnp.concatenate([held_ref[r, pair] for r in rows[c]], axis=0)
                top = jnp.concatenate([q_ref[c, :, at], none], axis=1)
                low = jnp.concatenate([none, up_ref[c, :, at]], axis=1)
                x = jnp.concatenate([top, low], axis=0)
                units.append((c, at, pair, held, x, nt(x, held)))
        mixed = []
        for c, at, pair, held, x, s in units:
            probs = softmax(s[:length] * scale)
            grad_probs = s[length:]
            total = jnp.sum(probs * grad_probs, axis=-1, keepdims=True)
            y = jnp.concatenate([probs * (grad_probs - total), probs], axis=0).astype(bf16)
            mixed.append((c, at, pair, held, x, y))
        for c, at, pair, held, x, y in mixed:
            z = nn(y, held)
            grad_ref[c, :, at] = (z[:length, :HS] * scale).astype(bf16)
            out_ref[c, :, at] = z[length:, HS:].astype(bf16)
            g = tn(y, x)
            g = jnp.concatenate([g[:, :HS] * scale, g[:, HS:]], axis=1).astype(bf16)
            for n in range(2):
                pairs_ref[rows[c][n], pair] = g[n * TOK : (n + 1) * TOK]
    sum_ref[...] = nn(turned_ref[...], pairs_ref[...]).astype(bf16)


def cross(slots, queries, upstream, weight, sources, per):
    spans, length, inner = queries.shape
    rows = len(sources) * TOK
    column = pl.BlockSpec((spans, length, per * HS), lambda i, s: (0, 0, i))
    return pl.pallas_call(
        functools.partial(cross_kernel, per),
        grid_spec=pltpu.PrefetchScalarGridSpec(
            num_scalar_prefetch=1,
            grid=(inner // HS // per,),
            in_specs=[
                column,
                column,
                pl.BlockSpec((ENC, 2 * HS * per), lambda i, s: (0, i)),
                *[pl.BlockSpec((TOK, ENC), lambda i, s: (0, 0))] * len(sources),
            ],
            out_specs=(
                column,
                column,
                pl.BlockSpec((rows, 2 * HS * per), lambda i, s: (0, i)),
                pl.BlockSpec((ENC, 2 * HS * per), lambda i, s: (0, i)),
            ),
            scratch_shapes=[
                pltpu.VMEM((rows, ENC), bf16),
                pltpu.VMEM((ENC, rows), bf16),
                pltpu.VMEM((rows, 2 * HS * per), bf16),
            ],
        ),
        out_shape=(
            jax.ShapeDtypeStruct(queries.shape, bf16),
            jax.ShapeDtypeStruct(queries.shape, bf16),
            jax.ShapeDtypeStruct((rows, 2 * inner), bf16),
            jax.ShapeDtypeStruct((ENC, 2 * inner), bf16),
        ),
        compiler_params=params(44, 1),
        cost_estimate=cost(16 * 10**9, 16 * 10**6),
    )(slots, queries, upstream, weight, *sources)


def place_kernel(sum_ref, out_ref):
    size, many = sum_ref.shape[0], sum_ref.shape[1] // HS
    for j in range(many):
        out_ref[pl.ds(j, size, stride=many), :] = sum_ref[:, j * HS : (j + 1) * HS].astype(f32)


def placed(summed):
    size = ENC // 4
    many = summed.shape[1] // HS
    return pl.pallas_call(
        place_kernel,
        grid=(4,),
        in_specs=[pl.BlockSpec((size, summed.shape[1]), lambda i: (i, 0))],
        out_specs=pl.BlockSpec((size * many, HS), lambda i: (i, 0)),
        out_shape=jax.ShapeDtypeStruct((ENC * many, HS), f32),
        compiler_params=params(16, 1),
        cost_estimate=cost(10**6, 11 * 10**6),
    )(summed)
def near_kernel(pairs_ref, weight_ref, brought_ref, own_ref, *outs):
    total = nt(pairs_ref[...], weight_ref[...]) + brought_ref[...].astype(f32)
    own_ref[...] = total[:TOK]
    for n, out in enumerate(outs):
        out[...] = total[(n + 1) * TOK : (n + 2) * TOK].astype(bf16)


def near_sums(pairs, weight, brought):
    def whole(*shape):
        return pl.BlockSpec(shape, lambda i: (0, 0))

    inner = weight.shape[1]
    return pl.pallas_call(
        near_kernel,
        grid=(1,),
        in_specs=[whole(4 * TOK, inner), whole(ENC, inner), whole(4 * TOK, ENC)],
        out_specs=[whole(TOK, ENC)] * 4,
        out_shape=[jax.ShapeDtypeStruct((TOK, ENC), f32)] + [jax.ShapeDtypeStruct((TOK, ENC), bf16)] * 3,
        compiler_params=params(32, 1),
        cost_estimate=cost(2 * 10**9, 8 * 10**6),
    )(pairs, weight, brought)


def columns_of(at):
    return at // LANES, slice(at % LANES, at % LANES + HS)


def backward_kernel(grad_ref, projected_ref, mix_ref, out_ref):
    grad = grad_ref[...]
    grad_mixed = nt(grad, mix_ref[...]).astype(bf16)
    heads = ENC // HS
    for j in range(PARTS * LANES // HS):
        part, lanes = columns_of(j * HS)
        if j < 3 * heads:
            continue
        near = j - 24
        if 0 <= near < heads:
            out_ref[part, :, lanes] = grad[:, near * HS : (near + 1) * HS]
        else:
            out_ref[part, :, lanes] = jnp.zeros((TOK, HS), bf16)
    for h in range(heads):
        q, k, v = (head(projected_ref, h, b) for b in range(3))
        g = grad_mixed[:, h * HS : (h + 1) * HS]
        probs = softmax(nt(q, k) / math.sqrt(HS))
        grad_probs = nt(g, v).astype(bf16).astype(f32)
        total = jnp.sum(probs * grad_probs, axis=-1, keepdims=True)
        grad_scores = (probs * (grad_probs - total) / math.sqrt(HS)).astype(bf16)
        for b, value in enumerate(
            (nn(grad_scores, k), tn(grad_scores, q), tn(probs.astype(bf16), g))
        ):
            part, lanes = columns_of(b * ENC + h * HS)
            out_ref[part, :, lanes] = value.astype(bf16)


def backward(grad, projected, mix):
    return pl.pallas_call(
        backward_kernel,
        out_shape=jax.ShapeDtypeStruct((PARTS, TOK, LANES), bf16),
        compiler_params=params(24),
        cost_estimate=cost(6 * 10**8, 4 * 10**6),
    )(grad, projected, mix)


def inputs_kernel(x_ref, gain_ref, project_ref, parts_ref, grad_ref, out_ref):
    many = 3 * ENC // LANES
    total = nt(parts_ref[0], project_ref[:, :LANES])
    for j in range(1, many):
        total += nt(parts_ref[j], project_ref[:, j * LANES : (j + 1) * LANES])
    rest = 3 * ENC - many * LANES
    total += nt(parts_ref[many][:, :rest], project_ref[:, many * LANES :])
    u = total.astype(bf16).astype(f32) * gain_ref[...]
    x = x_ref[...].astype(f32)
    r = lax.rsqrt(jnp.mean(x * x, axis=-1, keepdims=True) + epsilon)
    slope = jnp.mean(x * u, axis=-1, keepdims=True) * (r * r * r)
    out_ref[...] = (r * u - x * slope + grad_ref[...].astype(f32)).astype(bf16)


def inputs_grad(x, gain, project, parts, grad):
    return pl.pallas_call(
        inputs_kernel,
        out_shape=jax.ShapeDtypeStruct((TOK, ENC), bf16),
        compiler_params=params(24),
        cost_estimate=cost(6 * 10**8, 6 * 10**6),
    )(x, gain, project, parts, grad)


def shards(
    neighbour_inputs,
    encoder_gain,
    encoder_project,
    encoder_mix,
    decoder_queries,
    cross_pairs,
    span_neighbours,
    grad_output,
):
    gain = encoder_gain.reshape(1, ENC)
    y, core = lax.axis_index("y"), lax.axis_index("c")
    inner = cross_pairs.shape[2]
    heads = inner // HS
    weight = cross_pairs.reshape(ENC, 2, heads, HS).swapaxes(1, 2).reshape(ENC, 2 * inner)
    x, weight = lax.optimization_barrier((flipped(neighbour_inputs[0]), weight))
    encoded, normed, projected, mixed = encode(x, gain, encoder_project, encoder_mix)

    column = [encoded] + [turned("y", 4, -step)(encoded) for step in range(1, 4)]
    sources = column + [across(one) for one in column]
    operands, sources = lax.optimization_barrier((spread(normed, mixed), sources))
    operands = lax.all_gather(operands, TP, tiled=True)

    named = span_neighbours.reshape(-1) % 8
    slots = (named % 2 != core) * 4 + (named // 2 - y) % 4
    result, grad_queries, grad_pairs, grad_weight = cross(
        slots.astype(jnp.int32), decoder_queries, grad_output, weight, sources, heads
    )
    grad_cross = placed(lax.psum(grad_weight, PLANE))
    grad_cross = grad_cross.reshape(ENC, heads, 2, HS).swapaxes(1, 2).reshape(cross_pairs.shape)

    brought = across(nt(grad_pairs[4 * TOK :], weight).astype(bf16))
    total, *others = near_sums(grad_pairs, weight, brought)
    for step, other in enumerate(others):
        total += turned("y", 4, step + 1)(other).astype(f32)
    grad_encoded = total.astype(bf16)

    parts = backward(grad_encoded, projected, encoder_mix)
    all_parts = lax.all_to_all(parts, TP, 0, 0, tiled=True).reshape(8 * TOK, LANES)
    mine = jnp.where(y * 2 + core < 6, operands[:, :1024], operands[:, 1024:])
    encoder_grad = nn(lax.optimization_barrier(mine.T), all_parts).astype(bf16).reshape(128, 8, LANES)
    arrived = lax.all_to_all(encoder_grad, FINE, 0, 0, tiled=True).astype(f32)
    arrived = arrived.reshape(2, 8, 8, 8, LANES).sum(axis=(0, 2))
    rows = jnp.swapaxes(arrived, 0, 1).reshape(8, 8 * LANES)[:7]
    grad_inputs = flipped(inputs_grad(x, gain, encoder_project, parts, grad_encoded))
    return (
        result,
        grad_queries,
        grad_cross,
        rows[:, : 3 * ENC],
        rows[:, 6 * LANES : 6 * LANES + ENC],
        grad_inputs[None],
    )


def solution(mesh):
    fine = Mesh(mesh.devices.reshape(2, 4, 2, 2, 4), FINE)
    heads = P(PLANE, None, TP)
    placed = (
        P(FINE, None, None),
        P(),
        P(),
        P(),
        heads,
        P(None, None, TP),
        P(PLANE, None),
        heads,
    )
    return jax.shard_map(
        shards,
        mesh=fine,
        in_specs=placed,
        out_specs=(
            heads,
            heads,
            P(None, None, TP),
            P(FINE, None),
            P(FINE, None),
            P(FINE, None, None),
        ),
        check_vma=False,
    )
```

```python
import functools
import math

import jax
import jax.numpy as jnp
from jax import lax
from jax.experimental import pallas as pl
from jax.experimental.pallas import tpu as pltpu
from jax.sharding import Mesh
from jax.sharding import PartitionSpec as P

HS = 128
TOK = 128
ENC = 896
epsilon = 1e-06
f32 = jnp.float32
bf16 = jnp.bfloat16

FINE = ("xh", "y", "c", "xl", "z")
TP = ("y", "c")
PLANE = ("xh", "xl", "z")
LANES = 512
PARTS = 8


def turned(axis, length, by):
    pairs = [(i, (i + by) % length) for i in range(length)]
    return lambda x: lax.ppermute(x, axis, pairs)


def across(x):
    return lax.ppermute(x, "c", [(0, 1), (1, 0)])


def flipped(x):
    pairs = [(t * 8 + s, s * 8 + t) for t in range(8) for s in range(8)]
    return lax.ppermute(x, ("y", "c", "xl", "z"), pairs)


def dot(a, b, contract):
    return lax.dot_general(a, b, ((contract[:1], contract[1:]), ((), ())), preferred_element_type=f32)


def nn(a, b):
    return dot(a, b, (1, 0))


def nt(a, b):
    return dot(a, b, (1, 1))


def tn(a, b):
    return dot(a, b, (0, 0))


def params(mib, n=0):
    more = {"dimension_semantics": ("arbitrary",) * n} if n else {}
    return pltpu.CompilerParams(vmem_limit_bytes=mib * 2**20, **more)


def cost(flops, size):
    return pl.CostEstimate(flops=flops, bytes_accessed=size, transcendentals=0)


def softmax(scores):
    e = jnp.exp(scores - jnp.max(scores, axis=-1, keepdims=True))
    return e / jnp.sum(e, axis=-1, keepdims=True)


def head(ref, h, block=0):
    start = block * ENC + h * HS
    return ref[:, start : start + HS]


def encode_kernel(
    x_ref, gain_ref, project_ref, mix_ref, encoded_ref, normed_ref, projected_ref, mixed_ref, project, mix, sems
):
    thirds = [slice(b * ENC, (b + 1) * ENC) for b in range(3)]
    copies = [
        pltpu.make_async_copy(project_ref.at[:, at], project.at[:, at], sems.at[b])
        for b, at in enumerate(thirds)
    ]
    copies.append(pltpu.make_async_copy(mix_ref, mix, sems.at[3]))
    for copy in copies:
        copy.start()
    x = x_ref[...].astype(f32)
    r = lax.rsqrt(jnp.mean(x * x, axis=-1, keepdims=True) + epsilon)
    normed_ref[...] = (x * r * gain_ref[...]).astype(bf16)
    for b, at in enumerate(thirds):
        copies[b].wait()
        projected_ref[:, at] = nn(normed_ref[...], project[:, at]).astype(bf16)
    heads = range(ENC // HS)
    scores = [nt(head(projected_ref, h, 0), head(projected_ref, h, 1)) / math.sqrt(HS) for h in heads]
    weights = [softmax(s).astype(bf16) for s in scores]
    for h in heads:
        mixed_ref[:, h * HS : (h + 1) * HS] = nn(weights[h], head(projected_ref, h, 2)).astype(bf16)
    copies[3].wait()
    encoded_ref[...] = (x + nn(mixed_ref[...], mix[...])).astype(bf16)


def encode(x, gain, project, mix):
    shape = jax.ShapeDtypeStruct((TOK, ENC), bf16)
    wide = jax.ShapeDtypeStruct((TOK, 3 * ENC), bf16)
    vmem = pl.BlockSpec(memory_space=pltpu.VMEM)
    far = pl.BlockSpec(memory_space=pl.ANY)
    return pl.pallas_call(
        encode_kernel,
        in_specs=[vmem, vmem, far, far],
        out_specs=[vmem] * 4,
        out_shape=[shape, shape, wide, shape],
        scratch_shapes=[
            pltpu.VMEM((ENC, 3 * ENC), bf16),
            pltpu.VMEM((ENC, ENC), bf16),
            pltpu.SemaphoreType.DMA((4,)),
        ],
        compiler_params=params(58),
        cost_estimate=cost(10**9, 8 * 10**6),
    )(x, gain, project, mix)


def spread_kernel(normed_ref, mixed_ref, out_ref):
    column = lax.broadcasted_iota(jnp.int32, (ENC, 1024), 1)
    row = lax.broadcasted_iota(jnp.int32, (ENC, 1024), 0)
    place = jnp.where((column % 8 < 7) & (row == column // 8 * 7 + column % 8), 1.0, 0.0).astype(bf16)
    out_ref[:, :1024] = nn(normed_ref[...], place).astype(bf16)
    out_ref[:, 1024:] = nn(mixed_ref[...], place).astype(bf16)


def spread(normed, mixed):
    return pl.pallas_call(
        spread_kernel,
        out_shape=jax.ShapeDtypeStruct((TOK, 2048), bf16),
        compiler_params=params(24),
        cost_estimate=cost(5 * 10**8, 10**6),
    )(normed, mixed)


def cross_kernel(slots_ref, order_ref, q_ref, up_ref, far_weight_ref, *rest):
    sources, rest = rest[:8], rest[8:]
    (out_ref, grad_ref, sum_ref), blocks, far_ref, near = rest[:3], rest[3:7], rest[7], rest[8:12]
    weight_ref, rows_ref, turned_ref, held_ref, pairs_ref, sems = rest[12:]
    heads = weight_ref.shape[1] // (2 * HS)
    width = weight_ref.shape[1] // 4
    copies = []
    for j in range(4):
        at = slice(j * width, (j + 1) * width)
        copies.append(pltpu.make_async_copy(far_weight_ref.at[:, at], weight_ref.at[:, at], sems.at[j]))
    for copy in copies:
        copy.start()
    for n, source in enumerate(sources):
        rows_ref[n * TOK : (n + 1) * TOK] = source[...]
        turned_ref[:, n * TOK : (n + 1) * TOK] = source[...].T
    scale = 1.0 / math.sqrt(HS)
    length = q_ref.shape[1]
    none = jnp.zeros((length, HS), bf16)
    spans = range(q_ref.shape[0])
    rows = [
        [pl.ds(pl.multiple_of(slots_ref[2 * c + n] * TOK, TOK), TOK) for n in range(2)] for c in spans
    ]
    for j, copy in enumerate(copies):
        at = slice(j * width, (j + 1) * width)
        copy.wait()
        held_ref[:, at] = nn(rows_ref[...], weight_ref[:, at]).astype(bf16)
    for first in range(0, heads, 2):
        units = []
        for h in range(first, first + 2):
            at, pair = slice(h * HS, (h + 1) * HS), slice(2 * h * HS, 2 * (h + 1) * HS)
            for c in spans:
                held = jnp.concatenate([held_ref[r, pair] for r in rows[c]], axis=0)
                top = jnp.concatenate([q_ref[c, :, at], none], axis=1)
                low = jnp.concatenate([none, up_ref[c, :, at]], axis=1)
                x = jnp.concatenate([top, low], axis=0)
                units.append((c, at, pair, held, x, nt(x, held)))
        mixed = []
        for c, at, pair, held, x, s in units:
            probs = softmax(s[:length] * scale)
            grad_probs = s[length:]
            total = jnp.sum(probs * grad_probs, axis=-1, keepdims=True)
            y = jnp.concatenate([probs * (grad_probs - total), probs], axis=0).astype(bf16)
            mixed.append((c, at, pair, held, x, y))
        for c, at, pair, held, x, y in mixed:
            z = nn(y, held)
            grad_ref[c, :, at] = (z[:length, :HS] * scale).astype(bf16)
            out_ref[c, :, at] = z[length:, HS:].astype(bf16)
            g = tn(y, x)
            g = jnp.concatenate([g[:, :HS] * scale, g[:, HS:]], axis=1).astype(bf16)
            for n in range(2):
                pairs_ref[rows[c][n], pair] = g[n * TOK : (n + 1) * TOK]
    most = sum_ref.shape[1]
    sum_ref[...] = nn(turned_ref[...], pairs_ref[:, :most]).astype(bf16)
    for d, block in enumerate(blocks):
        at = pl.ds(pl.multiple_of(most + order_ref[d] * HS, HS), HS)
        block[...] = nn(turned_ref[...], pairs_ref[:, at]).astype(bf16)
    far_ref[...] = nt(pairs_ref[4 * TOK :], weight_ref[...]).astype(bf16)
    total = nt(pairs_ref[: 4 * TOK], weight_ref[...])
    for n, one in enumerate(near):
        one[...] = total[n * TOK : (n + 1) * TOK]


def cross(slots, order, queries, upstream, weight, sources):
    rows, wide = len(sources) * TOK, weight.shape[1]
    vmem = pl.BlockSpec(memory_space=pltpu.VMEM)
    smem = pl.BlockSpec(memory_space=pltpu.SMEM)
    return pl.pallas_call(
        cross_kernel,
        in_specs=[smem, smem, vmem, vmem, pl.BlockSpec(memory_space=pl.ANY)] + [vmem] * len(sources),
        out_specs=[vmem] * 12,
        out_shape=[
            jax.ShapeDtypeStruct(queries.shape, bf16),
            jax.ShapeDtypeStruct(queries.shape, bf16),
            jax.ShapeDtypeStruct((ENC, wide - 4 * HS), bf16),
            *[jax.ShapeDtypeStruct((ENC, HS), bf16)] * 4,
            jax.ShapeDtypeStruct((4 * TOK, ENC), bf16),
            *[jax.ShapeDtypeStruct((TOK, ENC), f32)] * 4,
        ],
        scratch_shapes=[
            pltpu.VMEM((ENC, wide), bf16),
            pltpu.VMEM((rows, ENC), bf16),
            pltpu.VMEM((ENC, rows), bf16),
            pltpu.VMEM((rows, wide), bf16),
            pltpu.VMEM((rows, wide), bf16),
            pltpu.SemaphoreType.DMA((4,)),
        ],
        compiler_params=params(50),
        cost_estimate=cost(24 * 10**9, 16 * 10**6),
    )(slots, order, queries, upstream, weight, *sources)


def plane_sum(blocks, first, second, at_second):
    total = blocks[0].astype(f32)
    for d in range(1, 4):
        total += turned(first, 4, d)(blocks[d]).astype(f32)
    total = total.astype(bf16)
    size = total.shape[0] // 4
    cuts = [lax.dynamic_slice_in_dim(total, (at_second + d) % 4 * size, size) for d in range(4)]
    piece = cuts[0].astype(f32)
    for d in range(1, 4):
        piece += turned(second, 4, d)(cuts[d]).astype(f32)
    piece = piece.astype(bf16)
    line = jnp.stack([piece] + [turned(second, 4, -d)(piece) for d in range(1, 4)])
    return [line] + [turned(first, 4, -d)(line) for d in range(1, 4)]


def place_kernel(at_ref, sum_ref, *rest):
    lines, out_ref = rest[:-1], rest[-1]
    size, most = sum_ref.shape[0], sum_ref.shape[1] // HS
    for j in range(most):
        out_ref[pl.ds(j, size, stride=most + 4), :] = sum_ref[:, j * HS : (j + 1) * HS].astype(f32)
    for h in range(4):
        for d in range(4):

            @pl.when((at_ref[0] + d) % 4 == h)
            def _():
                out_ref[pl.ds(most + h, size, stride=most + 4), :] = lines[d][0].astype(f32)


def placed(at, summed, lines):
    size, most = ENC // 4, summed.shape[1]
    many = most // HS + 4
    return pl.pallas_call(
        place_kernel,
        grid_spec=pltpu.PrefetchScalarGridSpec(
            num_scalar_prefetch=1,
            grid=(4,),
            in_specs=[
                pl.BlockSpec((size, most), lambda i, s: (i, 0)),
                *[pl.BlockSpec((1, size, HS), lambda i, s: ((i - s[1] + 4) % 4, 0, 0))] * 4,
            ],
            out_specs=pl.BlockSpec((size * many, HS), lambda i, s: (i, 0)),
        ),
        out_shape=jax.ShapeDtypeStruct((ENC * many, HS), f32),
        compiler_params=params(16, 1),
        cost_estimate=cost(10**6, 11 * 10**6),
    )(at, summed, *lines)


def turn_kernel(which_ref, held_ref, out_ref):
    at = pl.ds(pl.multiple_of(which_ref[0] * 1024, 1024), 1024)
    out_ref[...] = held_ref[:, at].T


def turned_operand(which, held):
    return pl.pallas_call(
        turn_kernel,
        in_specs=[pl.BlockSpec(memory_space=pltpu.SMEM), pl.BlockSpec(memory_space=pltpu.VMEM)],
        out_specs=pl.BlockSpec(memory_space=pltpu.VMEM),
        out_shape=jax.ShapeDtypeStruct((1024, held.shape[0]), bf16),
        compiler_params=params(24),
        cost_estimate=cost(10**4, 10**4),
    )(which, held)


def product_kernel(turned_ref, parts_ref, out_ref):
    out_ref[...] = nn(turned_ref[...], parts_ref[...]).astype(bf16)


def product(turned_rows, parts):
    return pl.pallas_call(
        product_kernel,
        out_shape=jax.ShapeDtypeStruct((turned_rows.shape[0], parts.shape[1]), bf16),
        compiler_params=params(24),
        cost_estimate=cost(10**4, 10**4),
    )(turned_rows, parts)


def columns_of(at):
    return at // LANES, slice(at % LANES, at % LANES + HS)


def backward_kernel(grad_ref, projected_ref, mix_ref, out_ref):
    grad = grad_ref[...]
    grad_mixed = nt(grad, mix_ref[...]).astype(bf16)
    heads = ENC // HS
    for j in range(PARTS * LANES // HS):
        part, lanes = columns_of(j * HS)
        if j < 3 * heads:
            continue
        near = j - 24
        if 0 <= near < heads:
            out_ref[part, :, lanes] = grad[:, near * HS : (near + 1) * HS]
        else:
            out_ref[part, :, lanes] = jnp.zeros((TOK, HS), bf16)
    for h in range(heads):
        q, k, v = (head(projected_ref, h, b) for b in range(3))
        g = grad_mixed[:, h * HS : (h + 1) * HS]
        probs = softmax(nt(q, k) / math.sqrt(HS))
        grad_probs = nt(g, v).astype(bf16).astype(f32)
        total = jnp.sum(probs * grad_probs, axis=-1, keepdims=True)
        grad_scores = (probs * (grad_probs - total) / math.sqrt(HS)).astype(bf16)
        for b, value in enumerate(
            (nn(grad_scores, k), tn(grad_scores, q), tn(probs.astype(bf16), g))
        ):
            part, lanes = columns_of(b * ENC + h * HS)
            out_ref[part, :, lanes] = value.astype(bf16)


def backward(grad, projected, mix):
    return pl.pallas_call(
        backward_kernel,
        out_shape=jax.ShapeDtypeStruct((PARTS, TOK, LANES), bf16),
        compiler_params=params(24),
        cost_estimate=cost(10**4, 10**4),
    )(grad, projected, mix)


def inputs_kernel(x_ref, gain_ref, project_ref, parts_ref, grad_ref, out_ref):
    many = 3 * ENC // LANES
    total = nt(parts_ref[0], project_ref[:, :LANES])
    for j in range(1, many):
        total += nt(parts_ref[j], project_ref[:, j * LANES : (j + 1) * LANES])
    rest = 3 * ENC - many * LANES
    total += nt(parts_ref[many][:, :rest], project_ref[:, many * LANES :])
    u = total.astype(bf16).astype(f32) * gain_ref[...]
    x = x_ref[...].astype(f32)
    r = lax.rsqrt(jnp.mean(x * x, axis=-1, keepdims=True) + epsilon)
    slope = jnp.mean(x * u, axis=-1, keepdims=True) * (r * r * r)
    out_ref[...] = (r * u - x * slope + grad_ref[...].astype(f32)).astype(bf16)


def inputs_grad(x, gain, project, parts, grad):
    return pl.pallas_call(
        inputs_kernel,
        out_shape=jax.ShapeDtypeStruct((TOK, ENC), bf16),
        compiler_params=params(24),
        cost_estimate=cost(10**4, 10**4),
    )(x, gain, project, parts, grad)


def shards(
    neighbour_inputs,
    encoder_gain,
    encoder_project,
    encoder_mix,
    decoder_queries,
    cross_pairs,
    span_neighbours,
    grad_output,
):
    gain = encoder_gain.reshape(1, ENC)
    y, core = lax.axis_index("y"), lax.axis_index("c")
    inner = cross_pairs.shape[2]
    heads = inner // HS
    weight = cross_pairs.reshape(ENC, 2, heads, HS).swapaxes(1, 2).reshape(ENC, 2 * inner)
    x, weight = lax.optimization_barrier((flipped(neighbour_inputs[0]), weight))
    encoded, normed, projected, mixed = encode(x, gain, encoder_project, encoder_mix)

    column = [encoded] + [turned("y", 4, -step)(encoded) for step in range(1, 4)]
    sources = column + [across(one) for one in column]
    operands, sources = lax.optimization_barrier((spread(normed, mixed), sources))
    operands = lax.all_gather(operands, TP, tiled=True)

    named = span_neighbours.reshape(-1) % 8
    slots = (named % 2 != core) * 4 + (named // 2 - y) % 4
    at_x = lax.axis_index("xh") * 2 + lax.axis_index("xl")
    at_z = lax.axis_index("z")
    order = (at_x + jnp.arange(4, dtype=jnp.int32)) % 4
    result, grad_queries, grad_weight, *rest = cross(
        slots.astype(jnp.int32), order, decoder_queries, grad_output, weight, sources
    )
    summed = lax.psum(grad_weight, PLANE)
    lines = plane_sum(rest[:4], ("xh", "xl"), "z", at_z)
    grad_cross = placed(jnp.stack([at_x, at_z]).astype(jnp.int32), summed, lines)
    grad_cross = grad_cross.reshape(ENC, heads, 2, HS).swapaxes(1, 2).reshape(cross_pairs.shape)

    brought = across(rest[4]).astype(f32)
    near = [one + brought[n * TOK : (n + 1) * TOK] for n, one in enumerate(rest[5:])]
    total = near[0]
    for step in range(1, 4):
        total += turned("y", 4, step)(near[step].astype(bf16)).astype(f32)
    grad_encoded = total.astype(bf16)

    parts = backward(grad_encoded, projected, encoder_mix)
    all_parts = lax.all_to_all(parts, TP, 0, 0, tiled=True).reshape(8 * TOK, LANES)
    which = (y * 2 + core >= 6).astype(jnp.int32).reshape(1)
    encoder_grad = product(turned_operand(which, operands), all_parts).reshape(128, 8, LANES)
    arrived = lax.all_to_all(encoder_grad, FINE, 0, 0, tiled=True).astype(f32)
    arrived = arrived.reshape(2, 8, 8, 8, LANES).sum(axis=(0, 2))
    rows = jnp.swapaxes(arrived, 0, 1).reshape(8, 8 * LANES)[:7]
    grad_inputs = flipped(inputs_grad(x, gain, encoder_project, parts, grad_encoded))
    return (
        result,
        grad_queries,
        grad_cross,
        rows[:, : 3 * ENC],
        rows[:, 6 * LANES : 6 * LANES + ENC],
        grad_inputs[None],
    )


def solution(mesh):
    fine = Mesh(mesh.devices.reshape(2, 4, 2, 2, 4), FINE)
    heads = P(PLANE, None, TP)
    placed = (
        P(FINE, None, None),
        P(),
        P(),
        P(),
        heads,
        P(None, None, TP),
        P(PLANE, None),
        heads,
    )
    return jax.shard_map(
        shards,
        mesh=fine,
        in_specs=placed,
        out_specs=(
            heads,
            heads,
            P(None, None, TP),
            P(FINE, None),
            P(FINE, None),
            P(FINE, None, None),
        ),
        check_vma=False,
    )
```

```python
import functools
import math

import jax
import jax.numpy as jnp
from jax import lax
from jax.experimental import pallas as pl
from jax.experimental.pallas import tpu as pltpu
from jax.sharding import Mesh
from jax.sharding import PartitionSpec as P

HS = 128
TOK = 128
ENC = 896
epsilon = 1e-06
f32 = jnp.float32
bf16 = jnp.bfloat16

FINE = ("xh", "y", "c", "xl", "z")
TP = ("y", "c")
PLANE = ("xh", "xl", "z")
LANES = 512
PARTS = 8


def turned(axis, length, by):
    pairs = [(i, (i + by) % length) for i in range(length)]
    return lambda x: lax.ppermute(x, axis, pairs)


def across(x):
    return lax.ppermute(x, "c", [(0, 1), (1, 0)])


def flipped(x):
    pairs = [(t * 8 + s, s * 8 + t) for t in range(8) for s in range(8)]
    return lax.ppermute(x, ("y", "c", "xl", "z"), pairs)


def dot(a, b, contract):
    return lax.dot_general(a, b, ((contract[:1], contract[1:]), ((), ())), preferred_element_type=f32)


def nn(a, b):
    return dot(a, b, (1, 0))


def nt(a, b):
    return dot(a, b, (1, 1))


def tn(a, b):
    return dot(a, b, (0, 0))


def params(mib, n=0):
    more = {"dimension_semantics": ("arbitrary",) * n} if n else {}
    return pltpu.CompilerParams(vmem_limit_bytes=mib * 2**20, **more)


def cost(flops, size):
    return pl.CostEstimate(flops=flops, bytes_accessed=size, transcendentals=0)


def softmax(scores):
    e = jnp.exp(scores - jnp.max(scores, axis=-1, keepdims=True))
    return e / jnp.sum(e, axis=-1, keepdims=True)


def head(ref, h, block=0):
    start = block * ENC + h * HS
    return ref[:, start : start + HS]


def encode_kernel(
    x_ref, gain_ref, project_ref, mix_ref, encoded_ref, normed_ref, projected_ref, mixed_ref, project, mix, sems
):
    thirds = [slice(b * ENC, (b + 1) * ENC) for b in range(3)]
    copies = [
        pltpu.make_async_copy(project_ref.at[:, at], project.at[:, at], sems.at[b])
        for b, at in enumerate(thirds)
    ]
    copies.append(pltpu.make_async_copy(mix_ref, mix, sems.at[3]))
    for copy in copies:
        copy.start()
    x = x_ref[...].astype(f32)
    r = lax.rsqrt(jnp.mean(x * x, axis=-1, keepdims=True) + epsilon)
    normed_ref[...] = (x * r * gain_ref[...]).astype(bf16)
    for b, at in enumerate(thirds):
        copies[b].wait()
        projected_ref[:, at] = nn(normed_ref[...], project[:, at]).astype(bf16)
    heads = range(ENC // HS)
    scores = [nt(head(projected_ref, h, 0), head(projected_ref, h, 1)) / math.sqrt(HS) for h in heads]
    weights = [softmax(s).astype(bf16) for s in scores]
    for h in heads:
        mixed_ref[:, h * HS : (h + 1) * HS] = nn(weights[h], head(projected_ref, h, 2)).astype(bf16)
    copies[3].wait()
    encoded_ref[...] = (x + nn(mixed_ref[...], mix[...])).astype(bf16)


def encode(x, gain, project, mix):
    shape = jax.ShapeDtypeStruct((TOK, ENC), bf16)
    wide = jax.ShapeDtypeStruct((TOK, 3 * ENC), bf16)
    vmem = pl.BlockSpec(memory_space=pltpu.VMEM)
    far = pl.BlockSpec(memory_space=pltpu.HBM)
    return pl.pallas_call(
        encode_kernel,
        in_specs=[vmem, vmem, far, far],
        out_specs=[vmem] * 4,
        out_shape=[shape, shape, wide, shape],
        scratch_shapes=[
            pltpu.VMEM((ENC, 3 * ENC), bf16),
            pltpu.VMEM((ENC, ENC), bf16),
            pltpu.SemaphoreType.DMA((4,)),
        ],
        compiler_params=params(24),
        cost_estimate=cost(10**9, 8 * 10**6),
    )(x, gain, project, mix)


def spread_kernel(normed_ref, mixed_ref, out_ref):
    column = lax.broadcasted_iota(jnp.int32, (ENC, 1024), 1)
    row = lax.broadcasted_iota(jnp.int32, (ENC, 1024), 0)
    place = jnp.where((column % 8 < 7) & (row == column // 8 * 7 + column % 8), 1.0, 0.0).astype(bf16)
    out_ref[:, :1024] = nn(normed_ref[...], place).astype(bf16)
    out_ref[:, 1024:] = nn(mixed_ref[...], place).astype(bf16)


def spread(normed, mixed):
    return pl.pallas_call(
        spread_kernel,
        out_shape=jax.ShapeDtypeStruct((TOK, 2048), bf16),
        compiler_params=params(24),
        cost_estimate=cost(5 * 10**8, 10**6),
    )(normed, mixed)


def cross_kernel(per, slots_ref, q_ref, up_ref, weight_ref, *rest):
    sources, (out_ref, grad_ref, pairs_ref, sum_ref, rows_ref, turned_ref, held_ref) = rest[:8], rest[8:]

    @pl.when(pl.program_id(0) == 0)
    def _():
        for n, source in enumerate(sources):
            rows_ref[n * TOK : (n + 1) * TOK] = source[...]
            turned_ref[:, n * TOK : (n + 1) * TOK] = source[...].T

    scale = 1.0 / math.sqrt(HS)
    length = q_ref.shape[1]
    none = jnp.zeros((length, HS), bf16)
    spans = range(q_ref.shape[0])
    rows = [
        [pl.ds(pl.multiple_of(slots_ref[2 * c + n] * TOK, TOK), TOK) for n in range(2)] for c in spans
    ]
    held_ref[...] = nn(rows_ref[...], weight_ref[...]).astype(bf16)
    for first in range(0, per, 2):
        units = []
        for h in range(first, first + 2):
            at, pair = slice(h * HS, (h + 1) * HS), slice(2 * h * HS, 2 * (h + 1) * HS)
            for c in spans:
                held = jnp.concatenate([held_ref[r, pair] for r in rows[c]], axis=0)
                top = jnp.concatenate([q_ref[c, :, at], none], axis=1)
                low = jnp.concatenate([none, up_ref[c, :, at]], axis=1)
                x = jnp.concatenate([top, low], axis=0)
                units.append((c, at, pair, held, x, nt(x, held)))
        mixed = []
        for c, at, pair, held, x, s in units:
            probs = softmax(s[:length] * scale)
            grad_probs = s[length:]
            total = jnp.sum(probs * grad_probs, axis=-1, keepdims=True)
            y = jnp.concatenate([probs * (grad_probs - total), probs], axis=0).astype(bf16)
            mixed.append((c, at, pair, held, x, y))
        for c, at, pair, held, x, y in mixed:
            z = nn(y, held)
            grad_ref[c, :, at] = (z[:length, :HS] * scale).astype(bf16)
            out_ref[c, :, at] = z[length:, HS:].astype(bf16)
            g = tn(y, x)
            g = jnp.concatenate([g[:, :HS] * scale, g[:, HS:]], axis=1).astype(bf16)
            for n in range(2):
                pairs_ref[rows[c][n], pair] = g[n * TOK : (n + 1) * TOK]
    sum_ref[...] = nn(turned_ref[...], pairs_ref[...]).astype(bf16)


def cross(slots, queries, upstream, weight, sources, per):
    spans, length, inner = queries.shape
    rows = len(sources) * TOK
    column = pl.BlockSpec((spans, length, per * HS), lambda i, s: (0, 0, i))
    return pl.pallas_call(
        functools.partial(cross_kernel, per),
        grid_spec=pltpu.PrefetchScalarGridSpec(
            num_scalar_prefetch=1,
            grid=(inner // HS // per,),
            in_specs=[
                column,
                column,
                pl.BlockSpec((ENC, 2 * HS * per), lambda i, s: (0, i)),
                *[pl.BlockSpec((TOK, ENC), lambda i, s: (0, 0))] * len(sources),
            ],
            out_specs=(
                column,
                column,
                pl.BlockSpec((rows, 2 * HS * per), lambda i, s: (0, i)),
                pl.BlockSpec((ENC, 2 * HS * per), lambda i, s: (0, i)),
            ),
            scratch_shapes=[
                pltpu.VMEM((rows, ENC), bf16),
                pltpu.VMEM((ENC, rows), bf16),
                pltpu.VMEM((rows, 2 * HS * per), bf16),
            ],
        ),
        out_shape=(
            jax.ShapeDtypeStruct(queries.shape, bf16),
            jax.ShapeDtypeStruct(queries.shape, bf16),
            jax.ShapeDtypeStruct((rows, 2 * inner), bf16),
            jax.ShapeDtypeStruct((ENC, 2 * inner), bf16),
        ),
        compiler_params=params(58, 1),
        cost_estimate=cost(16 * 10**9, 16 * 10**6),
    )(slots, queries, upstream, weight, *sources)


def place_kernel(sum_ref, out_ref):
    size, many = sum_ref.shape[0], sum_ref.shape[1] // HS
    out_ref[...] = sum_ref[...].astype(f32).reshape(size, many, HS).reshape(size * many, HS)


def placed(summed):
    size = ENC // 4
    many = summed.shape[1] // HS
    return pl.pallas_call(
        place_kernel,
        grid=(4,),
        in_specs=[pl.BlockSpec((size, summed.shape[1]), lambda i: (i, 0))],
        out_specs=pl.BlockSpec((size * many, HS), lambda i: (i, 0)),
        out_shape=jax.ShapeDtypeStruct((ENC * many, HS), f32),
        compiler_params=params(58, 1),
        cost_estimate=cost(10**6, 11 * 10**6),
    )(summed)


def near_kernel(pairs_ref, weight_ref, brought_ref, own_ref, *outs):
    total = nt(pairs_ref[...], weight_ref[...]) + brought_ref[...].astype(f32)
    own_ref[...] = total[:TOK]
    for n, out in enumerate(outs):
        out[...] = total[(n + 1) * TOK : (n + 2) * TOK].astype(bf16)


def near_sums(pairs, weight, brought):
    def whole(*shape):
        return pl.BlockSpec(shape, lambda i: (0, 0))

    inner = weight.shape[1]
    return pl.pallas_call(
        near_kernel,
        grid=(1,),
        in_specs=[whole(4 * TOK, inner), whole(ENC, inner), whole(4 * TOK, ENC)],
        out_specs=[whole(TOK, ENC)] * 4,
        out_shape=[jax.ShapeDtypeStruct((TOK, ENC), f32)] + [jax.ShapeDtypeStruct((TOK, ENC), bf16)] * 3,
        compiler_params=params(32, 1),
        cost_estimate=cost(10**4, 10**4),
    )(pairs, weight, brought)


def columns_of(at):
    return at // LANES, slice(at % LANES, at % LANES + HS)


def backward_kernel(grad_ref, projected_ref, mix_ref, out_ref):
    grad = grad_ref[...]
    grad_mixed = nt(grad, mix_ref[...]).astype(bf16)
    heads = ENC // HS
    for j in range(PARTS * LANES // HS):
        part, lanes = columns_of(j * HS)
        if j < 3 * heads:
            continue
        near = j - 24
        if 0 <= near < heads:
            out_ref[part, :, lanes] = grad[:, near * HS : (near + 1) * HS]
        else:
            out_ref[part, :, lanes] = jnp.zeros((TOK, HS), bf16)
    for h in range(heads):
        q, k, v = (head(projected_ref, h, b) for b in range(3))
        g = grad_mixed[:, h * HS : (h + 1) * HS]
        probs = softmax(nt(q, k) / math.sqrt(HS))
        grad_probs = nt(g, v).astype(bf16).astype(f32)
        total = jnp.sum(probs * grad_probs, axis=-1, keepdims=True)
        grad_scores = (probs * (grad_probs - total) / math.sqrt(HS)).astype(bf16)
        for b, value in enumerate(
            (nn(grad_scores, k), tn(grad_scores, q), tn(probs.astype(bf16), g))
        ):
            part, lanes = columns_of(b * ENC + h * HS)
            out_ref[part, :, lanes] = value.astype(bf16)


def backward(grad, projected, mix):
    return pl.pallas_call(
        backward_kernel,
        out_shape=jax.ShapeDtypeStruct((PARTS, TOK, LANES), bf16),
        compiler_params=params(24),
        cost_estimate=cost(10**4, 10**4),
    )(grad, projected, mix)


def inputs_kernel(x_ref, gain_ref, project_ref, parts_ref, grad_ref, out_ref):
    many = 3 * ENC // LANES
    total = nt(parts_ref[0], project_ref[:, :LANES])
    for j in range(1, many):
        total += nt(parts_ref[j], project_ref[:, j * LANES : (j + 1) * LANES])
    rest = 3 * ENC - many * LANES
    total += nt(parts_ref[many][:, :rest], project_ref[:, many * LANES :])
    u = total.astype(bf16).astype(f32) * gain_ref[...]
    x = x_ref[...].astype(f32)
    r = lax.rsqrt(jnp.mean(x * x, axis=-1, keepdims=True) + epsilon)
    slope = jnp.mean(x * u, axis=-1, keepdims=True) * (r * r * r)
    out_ref[...] = (r * u - x * slope + grad_ref[...].astype(f32)).astype(bf16)


def inputs_grad(x, gain, project, parts, grad):
    return pl.pallas_call(
        inputs_kernel,
        out_shape=jax.ShapeDtypeStruct((TOK, ENC), bf16),
        compiler_params=params(24),
        cost_estimate=cost(10**4, 10**4),
    )(x, gain, project, parts, grad)


def shards(
    neighbour_inputs,
    encoder_gain,
    encoder_project,
    encoder_mix,
    decoder_queries,
    cross_pairs,
    span_neighbours,
    grad_output,
):
    gain = encoder_gain.reshape(1, ENC)
    y, core = lax.axis_index("y"), lax.axis_index("c")
    inner = cross_pairs.shape[2]
    heads = inner // HS
    weight = cross_pairs.reshape(ENC, 2, heads, HS).swapaxes(1, 2).reshape(ENC, 2 * inner)
    x, weight = lax.optimization_barrier((flipped(neighbour_inputs[0]), weight))
    encoded, normed, projected, mixed = encode(x, gain, encoder_project, encoder_mix)

    column = [encoded] + [turned("y", 4, -step)(encoded) for step in range(1, 4)]
    sources = column + [across(one) for one in column]
    operands, sources = lax.optimization_barrier((spread(normed, mixed), sources))
    operands = lax.all_gather(operands, TP, tiled=True)

    named = span_neighbours.reshape(-1) % 8
    slots = (named % 2 != core) * 4 + (named // 2 - y) % 4
    result, grad_queries, grad_pairs, grad_weight = cross(
        slots.astype(jnp.int32), decoder_queries, grad_output, weight, sources, heads
    )
    summed = lax.psum(grad_weight, PLANE)

    brought = across(nt(grad_pairs[4 * TOK :], weight).astype(bf16))
    total, *others = near_sums(grad_pairs, weight, brought)
    for step, other in enumerate(others):
        total += turned("y", 4, step + 1)(other).astype(f32)
    grad_encoded = total.astype(bf16)

    parts = backward(grad_encoded, projected, encoder_mix)
    all_parts = lax.all_to_all(parts, TP, 0, 0, tiled=True).reshape(8 * TOK, LANES)
    mine = jnp.where(y * 2 + core < 6, operands[:, :1024], operands[:, 1024:])
    encoder_grad = nn(lax.optimization_barrier(mine.T), all_parts).astype(bf16).reshape(128, 8, LANES)
    arrived = lax.all_to_all(encoder_grad, FINE, 0, 0, tiled=True).astype(f32)
    arrived = arrived.reshape(2, 8, 8, 8, LANES).sum(axis=(0, 2))
    rows = jnp.swapaxes(arrived, 0, 1).reshape(8, 8 * LANES)[:7]
    grad_project, grad_mix = rows[:, : 3 * ENC], rows[:, 6 * LANES : 6 * LANES + ENC]
    grad_inputs = flipped(inputs_grad(x, gain, encoder_project, parts, grad_encoded))[None]
    summed, grad_project, grad_mix, grad_inputs = lax.optimization_barrier(
        (summed, grad_project, grad_mix, grad_inputs)
    )
    grad_cross = placed(summed).reshape(ENC, heads, 2, HS).swapaxes(1, 2).reshape(cross_pairs.shape)
    return result, grad_queries, grad_cross, grad_project, grad_mix, grad_inputs


def solution(mesh):
    fine = Mesh(mesh.devices.reshape(2, 4, 2, 2, 4), FINE)
    heads = P(PLANE, None, TP)
    placed = (
        P(FINE, None, None),
        P(),
        P(),
        P(),
        heads,
        P(None, None, TP),
        P(PLANE, None),
        heads,
    )
    return jax.shard_map(
        shards,
        mesh=fine,
        in_specs=placed,
        out_specs=(
            heads,
            heads,
            P(None, None, TP),
            P(FINE, None),
            P(FINE, None),
            P(FINE, None, None),
        ),
        check_vma=False,
    )
```

```python
import functools
import math

import jax
import jax.numpy as jnp
from jax import lax
from jax.experimental import pallas as pl
from jax.experimental.pallas import tpu as pltpu
from jax.sharding import Mesh
from jax.sharding import PartitionSpec as P

HS = 128
TOK = 128
ENC = 896
epsilon = 1e-06
f32 = jnp.float32
bf16 = jnp.bfloat16

FINE = ("xh", "y", "c", "xl", "z")
TP = ("y", "c")
PLANE = ("xh", "xl", "z")
LANES = 512
PARTS = 8


def turned(axis, length, by):
    pairs = [(i, (i + by) % length) for i in range(length)]
    return lambda x: lax.ppermute(x, axis, pairs)


def across(x):
    return lax.ppermute(x, "c", [(0, 1), (1, 0)])


def flipped(x):
    pairs = [(t * 8 + s, s * 8 + t) for t in range(8) for s in range(8)]
    return lax.ppermute(x, ("y", "c", "xl", "z"), pairs)


def dot(a, b, contract):
    return lax.dot_general(a, b, ((contract[:1], contract[1:]), ((), ())), preferred_element_type=f32)


def nn(a, b):
    return dot(a, b, (1, 0))


def nt(a, b):
    return dot(a, b, (1, 1))


def tn(a, b):
    return dot(a, b, (0, 0))


def params(mib, n=0):
    more = {"dimension_semantics": ("arbitrary",) * n} if n else {}
    return pltpu.CompilerParams(vmem_limit_bytes=mib * 2**20, **more)


def cost(flops, size):
    return pl.CostEstimate(flops=flops, bytes_accessed=size, transcendentals=0)


def softmax(scores):
    e = jnp.exp(scores - jnp.max(scores, axis=-1, keepdims=True))
    return e / jnp.sum(e, axis=-1, keepdims=True)


def head(ref, h, block=0):
    start = block * ENC + h * HS
    return ref[:, start : start + HS]


def encode_kernel(
    x_ref, gain_ref, project_ref, mix_ref, encoded_ref, normed_ref, projected_ref, mixed_ref, project, mix, sems
):
    thirds = [slice(b * ENC, (b + 1) * ENC) for b in range(3)]
    copies = [
        pltpu.make_async_copy(project_ref.at[:, at], project.at[:, at], sems.at[b])
        for b, at in enumerate(thirds)
    ]
    copies.append(pltpu.make_async_copy(mix_ref, mix, sems.at[3]))
    for copy in copies:
        copy.start()
    x = x_ref[...].astype(f32)
    r = lax.rsqrt(jnp.mean(x * x, axis=-1, keepdims=True) + epsilon)
    normed_ref[...] = (x * r * gain_ref[...]).astype(bf16)
    for b, at in enumerate(thirds):
        copies[b].wait()
        projected_ref[:, at] = nn(normed_ref[...], project[:, at]).astype(bf16)
    heads = range(ENC // HS)
    scores = [nt(head(projected_ref, h, 0), head(projected_ref, h, 1)) / math.sqrt(HS) for h in heads]
    weights = [softmax(s).astype(bf16) for s in scores]
    for h in heads:
        mixed_ref[:, h * HS : (h + 1) * HS] = nn(weights[h], head(projected_ref, h, 2)).astype(bf16)
    copies[3].wait()
    encoded_ref[...] = (x + nn(mixed_ref[...], mix[...])).astype(bf16)


def encode(x, gain, project, mix):
    shape = jax.ShapeDtypeStruct((TOK, ENC), bf16)
    wide = jax.ShapeDtypeStruct((TOK, 3 * ENC), bf16)
    vmem = pl.BlockSpec(memory_space=pltpu.VMEM)
    far = pl.BlockSpec(memory_space=pltpu.HBM)
    return pl.pallas_call(
        encode_kernel,
        in_specs=[vmem, vmem, far, far],
        out_specs=[vmem] * 4,
        out_shape=[shape, shape, wide, shape],
        scratch_shapes=[
            pltpu.VMEM((ENC, 3 * ENC), bf16),
            pltpu.VMEM((ENC, ENC), bf16),
            pltpu.SemaphoreType.DMA((4,)),
        ],
        compiler_params=params(24),
        cost_estimate=cost(10**9, 8 * 10**6),
    )(x, gain, project, mix)


def spread_kernel(normed_ref, mixed_ref, out_ref):
    column = lax.broadcasted_iota(jnp.int32, (ENC, 1024), 1)
    row = lax.broadcasted_iota(jnp.int32, (ENC, 1024), 0)
    place = jnp.where((column % 8 < 7) & (row == column // 8 * 7 + column % 8), 1.0, 0.0).astype(bf16)
    out_ref[:, :1024] = nn(normed_ref[...], place).astype(bf16)
    out_ref[:, 1024:] = nn(mixed_ref[...], place).astype(bf16)


def spread(normed, mixed):
    return pl.pallas_call(
        spread_kernel,
        out_shape=jax.ShapeDtypeStruct((TOK, 2048), bf16),
        compiler_params=params(24),
        cost_estimate=cost(5 * 10**8, 10**6),
    )(normed, mixed)


def cross_kernel(per, slots_ref, q_ref, up_ref, weight_ref, *rest):
    sources, rest = rest[:8], rest[8:]
    (out_ref, grad_ref, pairs_ref), halves, (rows_ref, turned_ref, held_ref) = rest[:3], rest[3:5], rest[5:]

    @pl.when(pl.program_id(0) == 0)
    def _():
        for n, source in enumerate(sources):
            rows_ref[n * TOK : (n + 1) * TOK] = source[...]
            turned_ref[:, n * TOK : (n + 1) * TOK] = source[...].T

    scale = 1.0 / math.sqrt(HS)
    length = q_ref.shape[1]
    none = jnp.zeros((length, HS), bf16)
    spans = range(q_ref.shape[0])
    rows = [
        [pl.ds(pl.multiple_of(slots_ref[2 * c + n] * TOK, TOK), TOK) for n in range(2)] for c in spans
    ]
    held_ref[...] = nn(rows_ref[...], weight_ref[...]).astype(bf16)
    for first in range(0, per, 2):
        units = []
        for h in range(first, first + 2):
            at, pair = slice(h * HS, (h + 1) * HS), slice(2 * h * HS, 2 * (h + 1) * HS)
            for c in spans:
                held = jnp.concatenate([held_ref[r, pair] for r in rows[c]], axis=0)
                top = jnp.concatenate([q_ref[c, :, at], none], axis=1)
                low = jnp.concatenate([none, up_ref[c, :, at]], axis=1)
                x = jnp.concatenate([top, low], axis=0)
                units.append((c, at, pair, held, x, nt(x, held)))
        mixed = []
        for c, at, pair, held, x, s in units:
            probs = softmax(s[:length] * scale)
            grad_probs = s[length:]
            total = jnp.sum(probs * grad_probs, axis=-1, keepdims=True)
            y = jnp.concatenate([probs * (grad_probs - total), probs], axis=0).astype(bf16)
            mixed.append((c, at, pair, held, x, y))
        for c, at, pair, held, x, y in mixed:
            z = nn(y, held)
            grad_ref[c, :, at] = (z[:length, :HS] * scale).astype(bf16)
            out_ref[c, :, at] = z[length:, HS:].astype(bf16)
            g = tn(y, x)
            g = jnp.concatenate([g[:, :HS] * scale, g[:, HS:]], axis=1).astype(bf16)
            for n in range(2):
                pairs_ref[rows[c][n], pair] = g[n * TOK : (n + 1) * TOK]
    for i, half in enumerate(halves):

        @pl.when(pl.program_id(0) == i)
        def _():
            half[...] = nn(turned_ref[...], pairs_ref[...]).astype(bf16)


def cross(slots, queries, upstream, weight, sources):
    per = queries.shape[2] // HS // 2
    spans, length, inner = queries.shape
    rows = len(sources) * TOK
    column = pl.BlockSpec((spans, length, per * HS), lambda i, s: (0, 0, i))
    return pl.pallas_call(
        functools.partial(cross_kernel, per),
        grid_spec=pltpu.PrefetchScalarGridSpec(
            num_scalar_prefetch=1,
            grid=(inner // HS // per,),
            in_specs=[
                column,
                column,
                pl.BlockSpec((ENC, 2 * HS * per), lambda i, s: (0, i)),
                *[pl.BlockSpec((TOK, ENC), lambda i, s: (0, 0))] * len(sources),
            ],
            out_specs=(
                column,
                column,
                pl.BlockSpec((rows, 2 * HS * per), lambda i, s: (0, i)),
                *[pl.BlockSpec((ENC, inner), lambda i, s: (0, 0))] * 2,
            ),
            scratch_shapes=[
                pltpu.VMEM((rows, ENC), bf16),
                pltpu.VMEM((ENC, rows), bf16),
                pltpu.VMEM((rows, 2 * HS * per), bf16),
            ],
        ),
        out_shape=(
            jax.ShapeDtypeStruct(queries.shape, bf16),
            jax.ShapeDtypeStruct(queries.shape, bf16),
            jax.ShapeDtypeStruct((rows, 2 * inner), bf16),
            *[jax.ShapeDtypeStruct((ENC, inner), bf16)] * 2,
        ),
        compiler_params=params(58, 1),
        cost_estimate=cost(16 * 10**9, 16 * 10**6),
    )(slots, queries, upstream, weight, *sources)


def place_kernel(one_ref, other_ref, out_ref):
    both = jnp.concatenate([one_ref[...], other_ref[...]], axis=1).astype(f32)
    size, many = both.shape[0], both.shape[1] // HS
    out_ref[...] = both.reshape(size, many, HS).reshape(size * many, HS)


def placed(one, other):
    size = ENC // 4
    many = (one.shape[1] + other.shape[1]) // HS
    return pl.pallas_call(
        place_kernel,
        grid=(4,),
        in_specs=[
            pl.BlockSpec((size, one.shape[1]), lambda i: (i, 0)),
            pl.BlockSpec((size, other.shape[1]), lambda i: (i, 0)),
        ],
        out_specs=pl.BlockSpec((size * many, HS), lambda i: (i, 0)),
        out_shape=jax.ShapeDtypeStruct((ENC * many, HS), f32),
        compiler_params=params(58, 1),
        cost_estimate=cost(10**6, 11 * 10**6),
    )(one, other)


def near_kernel(pairs_ref, weight_ref, brought_ref, own_ref, *outs):
    total = nt(pairs_ref[...], weight_ref[...]) + brought_ref[...].astype(f32)
    own_ref[...] = total[:TOK]
    for n, out in enumerate(outs):
        out[...] = total[(n + 1) * TOK : (n + 2) * TOK].astype(bf16)


def near_sums(pairs, weight, brought):
    def whole(*shape):
        return pl.BlockSpec(shape, lambda i: (0, 0))

    inner = weight.shape[1]
    return pl.pallas_call(
        near_kernel,
        grid=(1,),
        in_specs=[whole(4 * TOK, inner), whole(ENC, inner), whole(4 * TOK, ENC)],
        out_specs=[whole(TOK, ENC)] * 4,
        out_shape=[jax.ShapeDtypeStruct((TOK, ENC), f32)] + [jax.ShapeDtypeStruct((TOK, ENC), bf16)] * 3,
        compiler_params=params(32, 1),
        cost_estimate=cost(10**4, 10**4),
    )(pairs, weight, brought)


def columns_of(at):
    return at // LANES, slice(at % LANES, at % LANES + HS)


def backward_kernel(grad_ref, projected_ref, mix_ref, out_ref):
    grad = grad_ref[...]
    grad_mixed = nt(grad, mix_ref[...]).astype(bf16)
    heads = ENC // HS
    for j in range(PARTS * LANES // HS):
        part, lanes = columns_of(j * HS)
        if j < 3 * heads:
            continue
        near = j - 24
        if 0 <= near < heads:
            out_ref[part, :, lanes] = grad[:, near * HS : (near + 1) * HS]
        else:
            out_ref[part, :, lanes] = jnp.zeros((TOK, HS), bf16)
    for h in range(heads):
        q, k, v = (head(projected_ref, h, b) for b in range(3))
        g = grad_mixed[:, h * HS : (h + 1) * HS]
        probs = softmax(nt(q, k) / math.sqrt(HS))
        grad_probs = nt(g, v).astype(bf16).astype(f32)
        total = jnp.sum(probs * grad_probs, axis=-1, keepdims=True)
        grad_scores = (probs * (grad_probs - total) / math.sqrt(HS)).astype(bf16)
        for b, value in enumerate(
            (nn(grad_scores, k), tn(grad_scores, q), tn(probs.astype(bf16), g))
        ):
            part, lanes = columns_of(b * ENC + h * HS)
            out_ref[part, :, lanes] = value.astype(bf16)


def backward(grad, projected, mix):
    return pl.pallas_call(
        backward_kernel,
        out_shape=jax.ShapeDtypeStruct((PARTS, TOK, LANES), bf16),
        compiler_params=params(24),
        cost_estimate=cost(10**4, 10**4),
    )(grad, projected, mix)


def inputs_kernel(x_ref, gain_ref, project_ref, parts_ref, grad_ref, out_ref):
    many = 3 * ENC // LANES
    total = nt(parts_ref[0], project_ref[:, :LANES])
    for j in range(1, many):
        total += nt(parts_ref[j], project_ref[:, j * LANES : (j + 1) * LANES])
    rest = 3 * ENC - many * LANES
    total += nt(parts_ref[many][:, :rest], project_ref[:, many * LANES :])
    u = total.astype(bf16).astype(f32) * gain_ref[...]
    x = x_ref[...].astype(f32)
    r = lax.rsqrt(jnp.mean(x * x, axis=-1, keepdims=True) + epsilon)
    slope = jnp.mean(x * u, axis=-1, keepdims=True) * (r * r * r)
    out_ref[...] = (r * u - x * slope + grad_ref[...].astype(f32)).astype(bf16)


def inputs_grad(x, gain, project, parts, grad):
    return pl.pallas_call(
        inputs_kernel,
        out_shape=jax.ShapeDtypeStruct((TOK, ENC), bf16),
        compiler_params=params(24),
        cost_estimate=cost(10**4, 10**4),
    )(x, gain, project, parts, grad)


def shards(
    neighbour_inputs,
    encoder_gain,
    encoder_project,
    encoder_mix,
    decoder_queries,
    cross_pairs,
    span_neighbours,
    grad_output,
):
    gain = encoder_gain.reshape(1, ENC)
    y, core = lax.axis_index("y"), lax.axis_index("c")
    inner = cross_pairs.shape[2]
    heads = inner // HS
    weight = cross_pairs.reshape(ENC, 2, heads, HS).swapaxes(1, 2).reshape(ENC, 2 * inner)
    x, weight = lax.optimization_barrier((flipped(neighbour_inputs[0]), weight))
    encoded, normed, projected, mixed = encode(x, gain, encoder_project, encoder_mix)

    column = [encoded] + [turned("y", 4, -step)(encoded) for step in range(1, 4)]
    sources = column + [across(one) for one in column]
    operands, sources = lax.optimization_barrier((spread(normed, mixed), sources))
    operands = lax.all_gather(operands, TP, tiled=True)

    named = span_neighbours.reshape(-1) % 8
    slots = (named % 2 != core) * 4 + (named // 2 - y) % 4
    result, grad_queries, grad_pairs, one_half, other_half = cross(
        slots.astype(jnp.int32), decoder_queries, grad_output, weight, sources
    )
    one_half = lax.psum(one_half, PLANE)
    far = nt(grad_pairs[4 * TOK :], weight).astype(bf16)
    far, other_half = lax.optimization_barrier((far, other_half))
    brought = across(far)
    shares = lax.all_to_all(other_half.reshape(16, -1, inner), PLANE, 0, 0, tiled=True)

    total, *others = near_sums(grad_pairs, weight, brought)
    for step, other in enumerate(others):
        total += turned("y", 4, step + 1)(other).astype(f32)
    grad_encoded = total.astype(bf16)

    shares, _ = lax.optimization_barrier((shares, grad_encoded))
    share = jnp.sum(shares.astype(f32), axis=0).astype(bf16)
    other_half = lax.all_gather(share, PLANE, tiled=True)

    parts = backward(grad_encoded, projected, encoder_mix)
    all_parts = lax.all_to_all(parts, TP, 0, 0, tiled=True).reshape(8 * TOK, LANES)
    mine = jnp.where(y * 2 + core < 6, operands[:, :1024], operands[:, 1024:])
    encoder_grad = nn(lax.optimization_barrier(mine.T), all_parts).astype(bf16).reshape(128, 8, LANES)
    arrived = lax.all_to_all(encoder_grad, FINE, 0, 0, tiled=True).astype(f32)
    arrived = arrived.reshape(2, 8, 8, 8, LANES).sum(axis=(0, 2))
    rows = jnp.swapaxes(arrived, 0, 1).reshape(8, 8 * LANES)[:7]
    grad_project, grad_mix = rows[:, : 3 * ENC], rows[:, 6 * LANES : 6 * LANES + ENC]
    grad_inputs = flipped(inputs_grad(x, gain, encoder_project, parts, grad_encoded))[None]
    one_half, other_half, grad_project, grad_mix, grad_inputs = lax.optimization_barrier(
        (one_half, other_half, grad_project, grad_mix, grad_inputs)
    )
    grad_cross = placed(one_half, other_half).reshape(ENC, heads, 2, HS).swapaxes(1, 2).reshape(cross_pairs.shape)
    return result, grad_queries, grad_cross, grad_project, grad_mix, grad_inputs


def solution(mesh):
    fine = Mesh(mesh.devices.reshape(2, 4, 2, 2, 4), FINE)
    heads = P(PLANE, None, TP)
    placed = (
        P(FINE, None, None),
        P(),
        P(),
        P(),
        heads,
        P(None, None, TP),
        P(PLANE, None),
        heads,
    )
    return jax.shard_map(
        shards,
        mesh=fine,
        in_specs=placed,
        out_specs=(
            heads,
            heads,
            P(None, None, TP),
            P(FINE, None),
            P(FINE, None),
            P(FINE, None, None),
        ),
        check_vma=False,
    )
```

```python
import functools
import math

import jax
import jax.numpy as jnp
from jax import lax
from jax.experimental import pallas as pl
from jax.experimental.pallas import tpu as pltpu
from jax.sharding import Mesh
from jax.sharding import PartitionSpec as P

HS = 128
TOK = 128
ENC = 896
epsilon = 1e-06
f32 = jnp.float32
bf16 = jnp.bfloat16

FINE = ("xh", "y", "c", "xl", "z")
TP = ("y", "c")
PLANE = ("xh", "xl", "z")
LANES = 512
PARTS = 8


def turned(axis, length, by):
    pairs = [(i, (i + by) % length) for i in range(length)]
    return lambda x: lax.ppermute(x, axis, pairs)


def across(x):
    return lax.ppermute(x, "c", [(0, 1), (1, 0)])


def flipped(x):
    pairs = [(t * 8 + s, s * 8 + t) for t in range(8) for s in range(8)]
    return lax.ppermute(x, ("y", "c", "xl", "z"), pairs)


def dot(a, b, contract):
    return lax.dot_general(a, b, ((contract[:1], contract[1:]), ((), ())), preferred_element_type=f32)


def nn(a, b):
    return dot(a, b, (1, 0))


def nt(a, b):
    return dot(a, b, (1, 1))


def tn(a, b):
    return dot(a, b, (0, 0))


def params(mib, n=0):
    more = {"dimension_semantics": ("arbitrary",) * n} if n else {}
    return pltpu.CompilerParams(vmem_limit_bytes=mib * 2**20, **more)


def cost(flops, size):
    return pl.CostEstimate(flops=flops, bytes_accessed=size, transcendentals=0)


def softmax(scores):
    e = jnp.exp(scores - jnp.max(scores, axis=-1, keepdims=True))
    return e / jnp.sum(e, axis=-1, keepdims=True)


def head(ref, h, block=0):
    start = block * ENC + h * HS
    return ref[:, start : start + HS]


def encode_kernel(
    x_ref, gain_ref, project_ref, mix_ref, encoded_ref, normed_ref, projected_ref, mixed_ref, project, mix, sems
):
    thirds = [slice(b * ENC, (b + 1) * ENC) for b in range(3)]
    copies = [
        pltpu.make_async_copy(project_ref.at[:, at], project.at[:, at], sems.at[b])
        for b, at in enumerate(thirds)
    ]
    copies.append(pltpu.make_async_copy(mix_ref, mix, sems.at[3]))
    for copy in copies:
        copy.start()
    x = x_ref[...].astype(f32)
    r = lax.rsqrt(jnp.mean(x * x, axis=-1, keepdims=True) + epsilon)
    normed_ref[...] = (x * r * gain_ref[...]).astype(bf16)
    for b, at in enumerate(thirds):
        copies[b].wait()
        projected_ref[:, at] = nn(normed_ref[...], project[:, at]).astype(bf16)
    heads = range(ENC // HS)
    scores = [nt(head(projected_ref, h, 0), head(projected_ref, h, 1)) / math.sqrt(HS) for h in heads]
    weights = [softmax(s).astype(bf16) for s in scores]
    for h in heads:
        mixed_ref[:, h * HS : (h + 1) * HS] = nn(weights[h], head(projected_ref, h, 2)).astype(bf16)
    copies[3].wait()
    encoded_ref[...] = (x + nn(mixed_ref[...], mix[...])).astype(bf16)


def encode(x, gain, project, mix):
    shape = jax.ShapeDtypeStruct((TOK, ENC), bf16)
    wide = jax.ShapeDtypeStruct((TOK, 3 * ENC), bf16)
    vmem = pl.BlockSpec(memory_space=pltpu.VMEM)
    far = pl.BlockSpec(memory_space=pltpu.HBM)
    return pl.pallas_call(
        encode_kernel,
        in_specs=[vmem, vmem, far, far],
        out_specs=[vmem] * 4,
        out_shape=[shape, shape, wide, shape],
        scratch_shapes=[
            pltpu.VMEM((ENC, 3 * ENC), bf16),
            pltpu.VMEM((ENC, ENC), bf16),
            pltpu.SemaphoreType.DMA((4,)),
        ],
        compiler_params=params(24),
        cost_estimate=cost(10**9, 8 * 10**6),
    )(x, gain, project, mix)


def spread_kernel(normed_ref, mixed_ref, out_ref):
    column = lax.broadcasted_iota(jnp.int32, (ENC, 1024), 1)
    row = lax.broadcasted_iota(jnp.int32, (ENC, 1024), 0)
    place = jnp.where((column % 8 < 7) & (row == column // 8 * 7 + column % 8), 1.0, 0.0).astype(bf16)
    out_ref[:, :1024] = nn(normed_ref[...], place).astype(bf16)
    out_ref[:, 1024:] = nn(mixed_ref[...], place).astype(bf16)


def spread(normed, mixed):
    return pl.pallas_call(
        spread_kernel,
        out_shape=jax.ShapeDtypeStruct((TOK, 2048), bf16),
        compiler_params=params(24),
        cost_estimate=cost(5 * 10**8, 10**6),
    )(normed, mixed)


def cross_kernel(per, slots_ref, q_ref, up_ref, weight_ref, *rest):
    sources, rest = rest[:8], rest[8:]
    out_ref, grad_ref, pairs_ref, sum_ref, far_ref, rows_ref, turned_ref, held_ref = rest

    @pl.when(pl.program_id(0) == 0)
    def _():
        for n, source in enumerate(sources):
            rows_ref[n * TOK : (n + 1) * TOK] = source[...]
            turned_ref[:, n * TOK : (n + 1) * TOK] = source[...].T

    scale = 1.0 / math.sqrt(HS)
    length = q_ref.shape[1]
    none = jnp.zeros((length, HS), bf16)
    spans = range(q_ref.shape[0])
    rows = [
        [pl.ds(pl.multiple_of(slots_ref[2 * c + n] * TOK, TOK), TOK) for n in range(2)] for c in spans
    ]
    held_ref[...] = nn(rows_ref[...], weight_ref[...]).astype(bf16)
    for first in range(0, per, 2):
        units = []
        for h in range(first, first + 2):
            at, pair = slice(h * HS, (h + 1) * HS), slice(2 * h * HS, 2 * (h + 1) * HS)
            for c in spans:
                held = jnp.concatenate([held_ref[r, pair] for r in rows[c]], axis=0)
                top = jnp.concatenate([q_ref[c, :, at], none], axis=1)
                low = jnp.concatenate([none, up_ref[c, :, at]], axis=1)
                x = jnp.concatenate([top, low], axis=0)
                units.append((c, at, pair, held, x, nt(x, held)))
        mixed = []
        for c, at, pair, held, x, s in units:
            probs = softmax(s[:length] * scale)
            grad_probs = s[length:]
            total = jnp.sum(probs * grad_probs, axis=-1, keepdims=True)
            y = jnp.concatenate([probs * (grad_probs - total), probs], axis=0).astype(bf16)
            mixed.append((c, at, pair, held, x, y))
        for c, at, pair, held, x, y in mixed:
            z = nn(y, held)
            grad_ref[c, :, at] = (z[:length, :HS] * scale).astype(bf16)
            out_ref[c, :, at] = z[length:, HS:].astype(bf16)
            g = tn(y, x)
            g = jnp.concatenate([g[:, :HS] * scale, g[:, HS:]], axis=1).astype(bf16)
            for n in range(2):
                pairs_ref[rows[c][n], pair] = g[n * TOK : (n + 1) * TOK]
    sum_ref[...] = nn(turned_ref[...], pairs_ref[...]).astype(bf16)
    far_ref[...] = nt(pairs_ref[4 * TOK :], weight_ref[...]).astype(bf16)


def cross(slots, queries, upstream, weight, sources):
    spans, length, inner = queries.shape
    rows = len(sources) * TOK
    column = pl.BlockSpec((spans, length, inner), lambda i, s: (0, 0, i))
    return pl.pallas_call(
        functools.partial(cross_kernel, inner // HS),
        grid_spec=pltpu.PrefetchScalarGridSpec(
            num_scalar_prefetch=1,
            grid=(1,),
            in_specs=[
                column,
                column,
                pl.BlockSpec((ENC, 2 * inner), lambda i, s: (0, i)),
                *[pl.BlockSpec((TOK, ENC), lambda i, s: (0, 0))] * len(sources),
            ],
            out_specs=(
                column,
                column,
                pl.BlockSpec((rows, 2 * inner), lambda i, s: (0, i)),
                pl.BlockSpec((ENC, 2 * inner), lambda i, s: (0, i)),
                pl.BlockSpec((4 * TOK, ENC), lambda i, s: (0, 0)),
            ),
            scratch_shapes=[
                pltpu.VMEM((rows, ENC), bf16),
                pltpu.VMEM((ENC, rows), bf16),
                pltpu.VMEM((rows, 2 * inner), bf16),
            ],
        ),
        out_shape=(
            jax.ShapeDtypeStruct(queries.shape, bf16),
            jax.ShapeDtypeStruct(queries.shape, bf16),
            jax.ShapeDtypeStruct((rows, 2 * inner), bf16),
            jax.ShapeDtypeStruct((ENC, 2 * inner), bf16),
            jax.ShapeDtypeStruct((4 * TOK, ENC), bf16),
        ),
        compiler_params=params(58, 1),
        cost_estimate=cost(16 * 10**9, 16 * 10**6),
    )(slots, queries, upstream, weight, *sources)


def place_kernel(sum_ref, out_ref, held_ref, made_ref, sems):
    steps = 8
    size, many = sum_ref.shape[0] // steps, sum_ref.shape[1] // HS
    ins, outs = [], []
    for i in range(steps):
        at = slice(i * size, (i + 1) * size)
        ins.append(pltpu.make_async_copy(sum_ref.at[at], held_ref.at[at], sems.at[i]))
        ins[i].start()
    for i in range(steps):
        at, to = slice(i * size, (i + 1) * size), slice(i * size * many, (i + 1) * size * many)
        ins[i].wait()
        made_ref[to] = held_ref[at].astype(f32).reshape(size, many, HS).reshape(size * many, HS)
        outs.append(pltpu.make_async_copy(made_ref.at[to], out_ref.at[to], sems.at[steps + i]))
        outs[i].start()
    for copy in outs:
        copy.wait()


def placed(summed):
    many = summed.shape[1] // HS
    hbm = pl.BlockSpec(memory_space=pltpu.HBM)
    return pl.pallas_call(
        place_kernel,
        in_specs=[hbm],
        out_specs=hbm,
        out_shape=jax.ShapeDtypeStruct((ENC * many, HS), f32),
        scratch_shapes=[
            pltpu.VMEM(summed.shape, bf16),
            pltpu.VMEM((ENC * many, HS), f32),
            pltpu.SemaphoreType.DMA((16,)),
        ],
        compiler_params=params(58),
        cost_estimate=cost(10**6, 11 * 10**6),
    )(summed)


def near_kernel(pairs_ref, weight_ref, brought_ref, own_ref, *outs):
    total = nt(pairs_ref[...], weight_ref[...]) + brought_ref[...].astype(f32)
    own_ref[...] = total[:TOK]
    for n, out in enumerate(outs):
        out[...] = total[(n + 1) * TOK : (n + 2) * TOK].astype(bf16)


def near_sums(pairs, weight, brought):
    def whole(*shape):
        return pl.BlockSpec(shape, lambda i: (0, 0))

    inner = weight.shape[1]
    return pl.pallas_call(
        near_kernel,
        grid=(1,),
        in_specs=[whole(4 * TOK, inner), whole(ENC, inner), whole(4 * TOK, ENC)],
        out_specs=[whole(TOK, ENC)] * 4,
        out_shape=[jax.ShapeDtypeStruct((TOK, ENC), f32)] + [jax.ShapeDtypeStruct((TOK, ENC), bf16)] * 3,
        compiler_params=params(32, 1),
        cost_estimate=cost(10**4, 10**4),
    )(pairs, weight, brought)


def columns_of(at):
    return at // LANES, slice(at % LANES, at % LANES + HS)


def backward_kernel(grad_ref, projected_ref, mix_ref, out_ref):
    grad = grad_ref[...]
    grad_mixed = nt(grad, mix_ref[...]).astype(bf16)
    heads = ENC // HS
    for j in range(PARTS * LANES // HS):
        part, lanes = columns_of(j * HS)
        if j < 3 * heads:
            continue
        near = j - 24
        if 0 <= near < heads:
            out_ref[part, :, lanes] = grad[:, near * HS : (near + 1) * HS]
        else:
            out_ref[part, :, lanes] = jnp.zeros((TOK, HS), bf16)
    for h in range(heads):
        q, k, v = (head(projected_ref, h, b) for b in range(3))
        g = grad_mixed[:, h * HS : (h + 1) * HS]
        probs = softmax(nt(q, k) / math.sqrt(HS))
        grad_probs = nt(g, v).astype(bf16).astype(f32)
        total = jnp.sum(probs * grad_probs, axis=-1, keepdims=True)
        grad_scores = (probs * (grad_probs - total) / math.sqrt(HS)).astype(bf16)
        for b, value in enumerate(
            (nn(grad_scores, k), tn(grad_scores, q), tn(probs.astype(bf16), g))
        ):
            part, lanes = columns_of(b * ENC + h * HS)
            out_ref[part, :, lanes] = value.astype(bf16)


def backward(grad, projected, mix):
    return pl.pallas_call(
        backward_kernel,
        out_shape=jax.ShapeDtypeStruct((PARTS, TOK, LANES), bf16),
        compiler_params=params(24),
        cost_estimate=cost(10**4, 10**4),
    )(grad, projected, mix)


def inputs_kernel(x_ref, gain_ref, project_ref, parts_ref, grad_ref, out_ref):
    many = 3 * ENC // LANES
    total = nt(parts_ref[0], project_ref[:, :LANES])
    for j in range(1, many):
        total += nt(parts_ref[j], project_ref[:, j * LANES : (j + 1) * LANES])
    rest = 3 * ENC - many * LANES
    total += nt(parts_ref[many][:, :rest], project_ref[:, many * LANES :])
    u = total.astype(bf16).astype(f32) * gain_ref[...]
    x = x_ref[...].astype(f32)
    r = lax.rsqrt(jnp.mean(x * x, axis=-1, keepdims=True) + epsilon)
    slope = jnp.mean(x * u, axis=-1, keepdims=True) * (r * r * r)
    out_ref[...] = (r * u - x * slope + grad_ref[...].astype(f32)).astype(bf16)


def inputs_grad(x, gain, project, parts, grad):
    return pl.pallas_call(
        inputs_kernel,
        out_shape=jax.ShapeDtypeStruct((TOK, ENC), bf16),
        compiler_params=params(24),
        cost_estimate=cost(10**4, 10**4),
    )(x, gain, project, parts, grad)


def shards(
    neighbour_inputs,
    encoder_gain,
    encoder_project,
    encoder_mix,
    decoder_queries,
    cross_pairs,
    span_neighbours,
    grad_output,
):
    gain = encoder_gain.reshape(1, ENC)
    y, core = lax.axis_index("y"), lax.axis_index("c")
    inner = cross_pairs.shape[2]
    heads = inner // HS
    weight = cross_pairs.reshape(ENC, 2, heads, HS).swapaxes(1, 2).reshape(ENC, 2 * inner)
    x, weight = lax.optimization_barrier((flipped(neighbour_inputs[0]), weight))
    encoded, normed, projected, mixed = encode(x, gain, encoder_project, encoder_mix)

    column = [encoded] + [turned("y", 4, -step)(encoded) for step in range(1, 4)]
    sources = column + [across(one) for one in column]
    operands, sources = lax.optimization_barrier((spread(normed, mixed), sources))
    operands = lax.all_gather(operands, TP, tiled=True)

    named = span_neighbours.reshape(-1) % 8
    slots = (named % 2 != core) * 4 + (named // 2 - y) % 4
    result, grad_queries, grad_pairs, grad_weight, far = cross(
        slots.astype(jnp.int32), decoder_queries, grad_output, weight, sources
    )
    summed = lax.psum(grad_weight, PLANE)

    brought = across(far)
    total, *others = near_sums(grad_pairs, weight, brought)
    for step, other in enumerate(others):
        total += turned("y", 4, step + 1)(other).astype(f32)
    grad_encoded = total.astype(bf16)

    parts = backward(grad_encoded, projected, encoder_mix)
    all_parts = lax.all_to_all(parts, TP, 0, 0, tiled=True).reshape(8 * TOK, LANES)
    mine = jnp.where(y * 2 + core < 6, operands[:, :1024], operands[:, 1024:])
    encoder_grad = nn(lax.optimization_barrier(mine.T), all_parts).astype(bf16).reshape(128, 8, LANES)
    arrived = lax.all_to_all(encoder_grad, FINE, 0, 0, tiled=True).astype(f32)
    arrived = arrived.reshape(2, 8, 8, 8, LANES).sum(axis=(0, 2))
    rows = jnp.swapaxes(arrived, 0, 1).reshape(8, 8 * LANES)[:7]
    grad_project, grad_mix = rows[:, : 3 * ENC], rows[:, 6 * LANES : 6 * LANES + ENC]
    grad_inputs = flipped(inputs_grad(x, gain, encoder_project, parts, grad_encoded))[None]
    summed, grad_project, grad_mix, grad_inputs = lax.optimization_barrier(
        (summed, grad_project, grad_mix, grad_inputs)
    )
    grad_cross = placed(summed).reshape(ENC, heads, 2, HS).swapaxes(1, 2).reshape(cross_pairs.shape)
    return result, grad_queries, grad_cross, grad_project, grad_mix, grad_inputs


def solution(mesh):
    fine = Mesh(mesh.devices.reshape(2, 4, 2, 2, 4), FINE)
    heads = P(PLANE, None, TP)
    placed = (
        P(FINE, None, None),
        P(),
        P(),
        P(),
        heads,
        P(None, None, TP),
        P(PLANE, None),
        heads,
    )
    return jax.shard_map(
        shards,
        mesh=fine,
        in_specs=placed,
        out_specs=(
            heads,
            heads,
            P(None, None, TP),
            P(FINE, None),
            P(FINE, None),
            P(FINE, None, None),
        ),
        check_vma=False,
    )
```

```python
import functools
import math

import jax
import jax.numpy as jnp
from jax import lax
from jax.experimental import pallas as pl
from jax.experimental.pallas import tpu as pltpu
from jax.sharding import Mesh
from jax.sharding import PartitionSpec as P

HS = 128
TOK = 128
ENC = 896
epsilon = 1e-06
f32 = jnp.float32
bf16 = jnp.bfloat16

FINE = ("xh", "y", "c", "xl", "z")
TP = ("y", "c")
PLANE = ("xh", "xl", "z")
LANES = 512
PARTS = 8


def turned(axis, length, by):
    pairs = [(i, (i + by) % length) for i in range(length)]
    return lambda x: lax.ppermute(x, axis, pairs)


def across(x):
    return lax.ppermute(x, "c", [(0, 1), (1, 0)])


def flipped(x):
    pairs = [(t * 8 + s, s * 8 + t) for t in range(8) for s in range(8)]
    return lax.ppermute(x, ("y", "c", "xl", "z"), pairs)


def dot(a, b, contract):
    return lax.dot_general(a, b, ((contract[:1], contract[1:]), ((), ())), preferred_element_type=f32)


def nn(a, b):
    return dot(a, b, (1, 0))


def nt(a, b):
    return dot(a, b, (1, 1))


def tn(a, b):
    return dot(a, b, (0, 0))


def params(mib, n=0):
    more = {"dimension_semantics": ("arbitrary",) * n} if n else {}
    return pltpu.CompilerParams(vmem_limit_bytes=mib * 2**20, **more)


def cost(flops, size):
    return pl.CostEstimate(flops=flops, bytes_accessed=size, transcendentals=0)


def softmax(scores):
    e = jnp.exp(scores - jnp.max(scores, axis=-1, keepdims=True))
    return e / jnp.sum(e, axis=-1, keepdims=True)


def head(ref, h, block=0):
    start = block * ENC + h * HS
    return ref[:, start : start + HS]


def encode_kernel(
    x_ref, gain_ref, project_ref, mix_ref, encoded_ref, normed_ref, projected_ref, mixed_ref, project, mix, sems
):
    thirds = [slice(b * ENC, (b + 1) * ENC) for b in range(3)]
    copies = [
        pltpu.make_async_copy(project_ref.at[:, at], project.at[:, at], sems.at[b])
        for b, at in enumerate(thirds)
    ]
    copies.append(pltpu.make_async_copy(mix_ref, mix, sems.at[3]))
    for copy in copies:
        copy.start()
    x = x_ref[...].astype(f32)
    r = lax.rsqrt(jnp.mean(x * x, axis=-1, keepdims=True) + epsilon)
    normed_ref[...] = (x * r * gain_ref[...]).astype(bf16)
    for b, at in enumerate(thirds):
        copies[b].wait()
        projected_ref[:, at] = nn(normed_ref[...], project[:, at]).astype(bf16)
    heads = range(ENC // HS)
    scores = [nt(head(projected_ref, h, 0), head(projected_ref, h, 1)) / math.sqrt(HS) for h in heads]
    weights = [softmax(s).astype(bf16) for s in scores]
    for h in heads:
        mixed_ref[:, h * HS : (h + 1) * HS] = nn(weights[h], head(projected_ref, h, 2)).astype(bf16)
    copies[3].wait()
    encoded_ref[...] = (x + nn(mixed_ref[...], mix[...])).astype(bf16)


def encode(x, gain, project, mix):
    shape = jax.ShapeDtypeStruct((TOK, ENC), bf16)
    wide = jax.ShapeDtypeStruct((TOK, 3 * ENC), bf16)
    vmem = pl.BlockSpec(memory_space=pltpu.VMEM)
    far = pl.BlockSpec(memory_space=pltpu.HBM)
    return pl.pallas_call(
        encode_kernel,
        in_specs=[vmem, vmem, far, far],
        out_specs=[vmem] * 4,
        out_shape=[shape, shape, wide, shape],
        scratch_shapes=[
            pltpu.VMEM((ENC, 3 * ENC), bf16),
            pltpu.VMEM((ENC, ENC), bf16),
            pltpu.SemaphoreType.DMA((4,)),
        ],
        compiler_params=params(24),
        cost_estimate=cost(10**9, 8 * 10**6),
    )(x, gain, project, mix)


def spread_kernel(normed_ref, mixed_ref, out_ref):
    column = lax.broadcasted_iota(jnp.int32, (ENC, 1024), 1)
    row = lax.broadcasted_iota(jnp.int32, (ENC, 1024), 0)
    place = jnp.where((column % 8 < 7) & (row == column // 8 * 7 + column % 8), 1.0, 0.0).astype(bf16)
    out_ref[:, :1024] = nn(normed_ref[...], place).astype(bf16)
    out_ref[:, 1024:] = nn(mixed_ref[...], place).astype(bf16)


def spread(normed, mixed):
    return pl.pallas_call(
        spread_kernel,
        out_shape=jax.ShapeDtypeStruct((TOK, 2048), bf16),
        compiler_params=params(24),
        cost_estimate=cost(5 * 10**8, 10**6),
    )(normed, mixed)


def cross_kernel(per, slots_ref, q_ref, up_ref, weight_hbm, *rest):
    sources, (out_ref, grad_ref, pairs_hbm, sum_hbm, far_ref), rest = rest[:8], rest[8:13], rest[13:]
    weight_ref, rows_ref, turned_ref, held_ref, pairs_ref, sum_ref, sems = rest
    fetch = pltpu.make_async_copy(weight_hbm, weight_ref, sems.at[0])
    fetch.start()
    for n, source in enumerate(sources):
        rows_ref[n * TOK : (n + 1) * TOK] = source[...]
        turned_ref[:, n * TOK : (n + 1) * TOK] = source[...].T
    fetch.wait()
    scale = 1.0 / math.sqrt(HS)
    length = q_ref.shape[1]
    none = jnp.zeros((length, HS), bf16)
    spans = range(q_ref.shape[0])
    rows = [
        [pl.ds(pl.multiple_of(slots_ref[2 * c + n] * TOK, TOK), TOK) for n in range(2)] for c in spans
    ]
    held_ref[...] = nn(rows_ref[...], weight_ref[...]).astype(bf16)
    for first in range(0, per, 2):
        units = []
        for h in range(first, first + 2):
            at, pair = slice(h * HS, (h + 1) * HS), slice(2 * h * HS, 2 * (h + 1) * HS)
            for c in spans:
                held = jnp.concatenate([held_ref[r, pair] for r in rows[c]], axis=0)
                top = jnp.concatenate([q_ref[c, :, at], none], axis=1)
                low = jnp.concatenate([none, up_ref[c, :, at]], axis=1)
                x = jnp.concatenate([top, low], axis=0)
                units.append((c, at, pair, held, x, nt(x, held)))
        mixed = []
        for c, at, pair, held, x, s in units:
            probs = softmax(s[:length] * scale)
            grad_probs = s[length:]
            total = jnp.sum(probs * grad_probs, axis=-1, keepdims=True)
            y = jnp.concatenate([probs * (grad_probs - total), probs], axis=0).astype(bf16)
            mixed.append((c, at, pair, held, x, y))
        for c, at, pair, held, x, y in mixed:
            z = nn(y, held)
            grad_ref[c, :, at] = (z[:length, :HS] * scale).astype(bf16)
            out_ref[c, :, at] = z[length:, HS:].astype(bf16)
            g = tn(y, x)
            g = jnp.concatenate([g[:, :HS] * scale, g[:, HS:]], axis=1).astype(bf16)
            for n in range(2):
                pairs_ref[rows[c][n], pair] = g[n * TOK : (n + 1) * TOK]
    give_pairs = pltpu.make_async_copy(pairs_ref, pairs_hbm, sems.at[1])
    give_pairs.start()
    sum_ref[...] = nn(turned_ref[...], pairs_ref[...]).astype(bf16)
    give_sum = pltpu.make_async_copy(sum_ref, sum_hbm, sems.at[2])
    give_sum.start()
    far_ref[...] = nt(pairs_ref[4 * TOK :], weight_ref[...]).astype(bf16)
    give_pairs.wait()
    give_sum.wait()


def cross(slots, queries, upstream, weight, sources):
    spans, length, inner = queries.shape
    rows = len(sources) * TOK
    column = pl.BlockSpec((spans, length, inner), lambda i, s: (0, 0, i))
    hbm = pl.BlockSpec(memory_space=pltpu.HBM)
    return pl.pallas_call(
        functools.partial(cross_kernel, inner // HS),
        grid_spec=pltpu.PrefetchScalarGridSpec(
            num_scalar_prefetch=1,
            grid=(1,),
            in_specs=[
                column,
                column,
                hbm,
                *[pl.BlockSpec((TOK, ENC), lambda i, s: (0, 0))] * len(sources),
            ],
            out_specs=(
                column,
                column,
                hbm,
                hbm,
                pl.BlockSpec((4 * TOK, ENC), lambda i, s: (0, 0)),
            ),
            scratch_shapes=[
                pltpu.VMEM((ENC, 2 * inner), bf16),
                pltpu.VMEM((rows, ENC), bf16),
                pltpu.VMEM((ENC, rows), bf16),
                pltpu.VMEM((rows, 2 * inner), bf16),
                pltpu.VMEM((rows, 2 * inner), bf16),
                pltpu.VMEM((ENC, 2 * inner), bf16),
                pltpu.SemaphoreType.DMA((3,)),
            ],
        ),
        out_shape=(
            jax.ShapeDtypeStruct(queries.shape, bf16),
            jax.ShapeDtypeStruct(queries.shape, bf16),
            jax.ShapeDtypeStruct((rows, 2 * inner), bf16),
            jax.ShapeDtypeStruct((ENC, 2 * inner), bf16),
            jax.ShapeDtypeStruct((4 * TOK, ENC), bf16),
        ),
        compiler_params=params(58, 1),
        cost_estimate=cost(16 * 10**9, 16 * 10**6),
    )(slots, queries, upstream, weight, *sources)


def place_kernel(sum_ref, out_ref, held_ref, made_ref, sems):
    steps = 8
    size, many = sum_ref.shape[0] // steps, sum_ref.shape[1] // HS
    ins, outs = [], []
    for i in range(steps):
        at = slice(i * size, (i + 1) * size)
        ins.append(pltpu.make_async_copy(sum_ref.at[at], held_ref.at[at], sems.at[i]))
        ins[i].start()
    for i in range(steps):
        at, to = slice(i * size, (i + 1) * size), slice(i * size * many, (i + 1) * size * many)
        ins[i].wait()
        made_ref[to] = held_ref[at].astype(f32).reshape(size, many, HS).reshape(size * many, HS)
        outs.append(pltpu.make_async_copy(made_ref.at[to], out_ref.at[to], sems.at[steps + i]))
        outs[i].start()
    for copy in outs:
        copy.wait()


def placed(summed):
    many = summed.shape[1] // HS
    hbm = pl.BlockSpec(memory_space=pltpu.HBM)
    return pl.pallas_call(
        place_kernel,
        in_specs=[hbm],
        out_specs=hbm,
        out_shape=jax.ShapeDtypeStruct((ENC * many, HS), f32),
        scratch_shapes=[
            pltpu.VMEM(summed.shape, bf16),
            pltpu.VMEM((ENC * many, HS), f32),
            pltpu.SemaphoreType.DMA((16,)),
        ],
        compiler_params=params(58),
        cost_estimate=cost(10**6, 11 * 10**6),
    )(summed)


def near_kernel(pairs_ref, weight_ref, brought_ref, own_ref, *outs):
    total = nt(pairs_ref[...], weight_ref[...]) + brought_ref[...].astype(f32)
    own_ref[...] = total[:TOK]
    for n, out in enumerate(outs):
        out[...] = total[(n + 1) * TOK : (n + 2) * TOK].astype(bf16)


def near_sums(pairs, weight, brought):
    def whole(*shape):
        return pl.BlockSpec(shape, lambda i: (0, 0))

    inner = weight.shape[1]
    return pl.pallas_call(
        near_kernel,
        grid=(1,),
        in_specs=[whole(4 * TOK, inner), whole(ENC, inner), whole(4 * TOK, ENC)],
        out_specs=[whole(TOK, ENC)] * 4,
        out_shape=[jax.ShapeDtypeStruct((TOK, ENC), f32)] + [jax.ShapeDtypeStruct((TOK, ENC), bf16)] * 3,
        compiler_params=params(32, 1),
        cost_estimate=cost(10**4, 10**4),
    )(pairs, weight, brought)


def columns_of(at):
    return at // LANES, slice(at % LANES, at % LANES + HS)


def backward_kernel(grad_ref, projected_ref, mix_ref, out_ref):
    grad = grad_ref[...]
    grad_mixed = nt(grad, mix_ref[...]).astype(bf16)
    heads = ENC // HS
    for j in range(PARTS * LANES // HS):
        part, lanes = columns_of(j * HS)
        if j < 3 * heads:
            continue
        near = j - 24
        if 0 <= near < heads:
            out_ref[part, :, lanes] = grad[:, near * HS : (near + 1) * HS]
        else:
            out_ref[part, :, lanes] = jnp.zeros((TOK, HS), bf16)
    for h in range(heads):
        q, k, v = (head(projected_ref, h, b) for b in range(3))
        g = grad_mixed[:, h * HS : (h + 1) * HS]
        probs = softmax(nt(q, k) / math.sqrt(HS))
        grad_probs = nt(g, v).astype(bf16).astype(f32)
        total = jnp.sum(probs * grad_probs, axis=-1, keepdims=True)
        grad_scores = (probs * (grad_probs - total) / math.sqrt(HS)).astype(bf16)
        for b, value in enumerate(
            (nn(grad_scores, k), tn(grad_scores, q), tn(probs.astype(bf16), g))
        ):
            part, lanes = columns_of(b * ENC + h * HS)
            out_ref[part, :, lanes] = value.astype(bf16)


def backward(grad, projected, mix):
    return pl.pallas_call(
        backward_kernel,
        out_shape=jax.ShapeDtypeStruct((PARTS, TOK, LANES), bf16),
        compiler_params=params(24),
        cost_estimate=cost(10**4, 10**4),
    )(grad, projected, mix)


def inputs_kernel(x_ref, gain_ref, project_ref, parts_ref, grad_ref, out_ref):
    many = 3 * ENC // LANES
    total = nt(parts_ref[0], project_ref[:, :LANES])
    for j in range(1, many):
        total += nt(parts_ref[j], project_ref[:, j * LANES : (j + 1) * LANES])
    rest = 3 * ENC - many * LANES
    total += nt(parts_ref[many][:, :rest], project_ref[:, many * LANES :])
    u = total.astype(bf16).astype(f32) * gain_ref[...]
    x = x_ref[...].astype(f32)
    r = lax.rsqrt(jnp.mean(x * x, axis=-1, keepdims=True) + epsilon)
    slope = jnp.mean(x * u, axis=-1, keepdims=True) * (r * r * r)
    out_ref[...] = (r * u - x * slope + grad_ref[...].astype(f32)).astype(bf16)


def inputs_grad(x, gain, project, parts, grad):
    return pl.pallas_call(
        inputs_kernel,
        out_shape=jax.ShapeDtypeStruct((TOK, ENC), bf16),
        compiler_params=params(24),
        cost_estimate=cost(10**4, 10**4),
    )(x, gain, project, parts, grad)


def shards(
    neighbour_inputs,
    encoder_gain,
    encoder_project,
    encoder_mix,
    decoder_queries,
    cross_pairs,
    span_neighbours,
    grad_output,
):
    gain = encoder_gain.reshape(1, ENC)
    y, core = lax.axis_index("y"), lax.axis_index("c")
    inner = cross_pairs.shape[2]
    heads = inner // HS
    weight = cross_pairs.reshape(ENC, 2, heads, HS).swapaxes(1, 2).reshape(ENC, 2 * inner)
    x, weight = lax.optimization_barrier((flipped(neighbour_inputs[0]), weight))
    encoded, normed, projected, mixed = encode(x, gain, encoder_project, encoder_mix)

    column = [encoded] + [turned("y", 4, -step)(encoded) for step in range(1, 4)]
    sources = column + [across(one) for one in column]
    operands, sources = lax.optimization_barrier((spread(normed, mixed), sources))
    operands = lax.all_gather(operands, TP, tiled=True)

    named = span_neighbours.reshape(-1) % 8
    slots = (named % 2 != core) * 4 + (named // 2 - y) % 4
    result, grad_queries, grad_pairs, grad_weight, far = cross(
        slots.astype(jnp.int32), decoder_queries, grad_output, weight, sources
    )
    summed = lax.psum(grad_weight, PLANE)

    brought = across(far)
    total, *others = near_sums(grad_pairs, weight, brought)
    for step, other in enumerate(others):
        total += turned("y", 4, step + 1)(other).astype(f32)
    grad_encoded = total.astype(bf16)

    parts = backward(grad_encoded, projected, encoder_mix)
    all_parts = lax.all_to_all(parts, TP, 0, 0, tiled=True).reshape(8 * TOK, LANES)
    mine = jnp.where(y * 2 + core < 6, operands[:, :1024], operands[:, 1024:])
    encoder_grad = nn(lax.optimization_barrier(mine.T), all_parts).astype(bf16).reshape(128, 8, LANES)
    arrived = lax.all_to_all(encoder_grad, FINE, 0, 0, tiled=True).astype(f32)
    arrived = arrived.reshape(2, 8, 8, 8, LANES).sum(axis=(0, 2))
    rows = jnp.swapaxes(arrived, 0, 1).reshape(8, 8 * LANES)[:7]
    grad_project, grad_mix = rows[:, : 3 * ENC], rows[:, 6 * LANES : 6 * LANES + ENC]
    grad_inputs = flipped(inputs_grad(x, gain, encoder_project, parts, grad_encoded))[None]
    summed, grad_project, grad_mix, grad_inputs = lax.optimization_barrier(
        (summed, grad_project, grad_mix, grad_inputs)
    )
    grad_cross = placed(summed).reshape(ENC, heads, 2, HS).swapaxes(1, 2).reshape(cross_pairs.shape)
    return result, grad_queries, grad_cross, grad_project, grad_mix, grad_inputs


def solution(mesh):
    fine = Mesh(mesh.devices.reshape(2, 4, 2, 2, 4), FINE)
    heads = P(PLANE, None, TP)
    placed = (
        P(FINE, None, None),
        P(),
        P(),
        P(),
        heads,
        P(None, None, TP),
        P(PLANE, None),
        heads,
    )
    return jax.shard_map(
        shards,
        mesh=fine,
        in_specs=placed,
        out_specs=(
            heads,
            heads,
            P(None, None, TP),
            P(FINE, None),
            P(FINE, None),
            P(FINE, None, None),
        ),
        check_vma=False,
    )
```

```python
import functools
import math

import jax
import jax.numpy as jnp
from jax import lax
from jax.experimental import pallas as pl
from jax.experimental.pallas import tpu as pltpu
from jax.sharding import Mesh
from jax.sharding import PartitionSpec as P

HS = 128
TOK = 128
ENC = 896
epsilon = 1e-06
f32 = jnp.float32
bf16 = jnp.bfloat16

FINE = ("xh", "y", "c", "xl", "z")
TP = ("y", "c")
PLANE = ("xh", "xl", "z")
LANES = 512
PARTS = 8


def across(x):
    return lax.ppermute(x, "c", [(0, 1), (1, 0)])


def routes(step):
    return [
        (t * 8 + s, ((s // 2 - step) % 4 * 2 + s % 2) * 8 + t) for t in range(8) for s in range(8)
    ]


def sent(x, step):
    return lax.ppermute(x, ("y", "c", "xl", "z"), routes(step))


def sent_back(x, step):
    return lax.ppermute(x, ("y", "c", "xl", "z"), [(b, a) for a, b in routes(step)])


def dot(a, b, contract):
    return lax.dot_general(a, b, ((contract[:1], contract[1:]), ((), ())), preferred_element_type=f32)


def nn(a, b):
    return dot(a, b, (1, 0))


def nt(a, b):
    return dot(a, b, (1, 1))


def tn(a, b):
    return dot(a, b, (0, 0))


def params(mib, n=0):
    more = {"dimension_semantics": ("arbitrary",) * n} if n else {}
    return pltpu.CompilerParams(vmem_limit_bytes=mib * 2**20, **more)


def cost(flops, size):
    return pl.CostEstimate(flops=flops, bytes_accessed=size, transcendentals=0)


def softmax(scores):
    e = jnp.exp(scores - jnp.max(scores, axis=-1, keepdims=True))
    return e / jnp.sum(e, axis=-1, keepdims=True)


def head(ref, h, block=0):
    start = block * ENC + h * HS
    return ref[:, start : start + HS]


def encode_kernel(
    x_ref, gain_ref, project_ref, mix_ref, encoded_ref, normed_ref, projected_ref, mixed_ref, project, mix, sems
):
    thirds = [slice(b * ENC, (b + 1) * ENC) for b in range(3)]
    copies = [
        pltpu.make_async_copy(project_ref.at[:, at], project.at[:, at], sems.at[b])
        for b, at in enumerate(thirds)
    ]
    copies.append(pltpu.make_async_copy(mix_ref, mix, sems.at[3]))
    for copy in copies:
        copy.start()
    x = x_ref[...].astype(f32)
    r = lax.rsqrt(jnp.mean(x * x, axis=-1, keepdims=True) + epsilon)
    normed_ref[...] = (x * r * gain_ref[...]).astype(bf16)
    for b, at in enumerate(thirds):
        copies[b].wait()
        projected_ref[:, at] = nn(normed_ref[...], project[:, at]).astype(bf16)
    heads = range(ENC // HS)
    scores = [nt(head(projected_ref, h, 0), head(projected_ref, h, 1)) / math.sqrt(HS) for h in heads]
    weights = [softmax(s).astype(bf16) for s in scores]
    for h in heads:
        mixed_ref[:, h * HS : (h + 1) * HS] = nn(weights[h], head(projected_ref, h, 2)).astype(bf16)
    copies[3].wait()
    encoded_ref[...] = (x + nn(mixed_ref[...], mix[...])).astype(bf16)


def encode(x, gain, project, mix):
    shape = jax.ShapeDtypeStruct((TOK, ENC), bf16)
    wide = jax.ShapeDtypeStruct((TOK, 3 * ENC), bf16)
    vmem = pl.BlockSpec(memory_space=pltpu.VMEM)
    far = pl.BlockSpec(memory_space=pltpu.HBM)
    return pl.pallas_call(
        encode_kernel,
        in_specs=[vmem, vmem, far, far],
        out_specs=[vmem] * 4,
        out_shape=[shape, shape, wide, shape],
        scratch_shapes=[
            pltpu.VMEM((ENC, 3 * ENC), bf16),
            pltpu.VMEM((ENC, ENC), bf16),
            pltpu.SemaphoreType.DMA((4,)),
        ],
        compiler_params=params(24),
        cost_estimate=cost(10**9, 8 * 10**6),
    )(x, gain, project, mix)


def spread_kernel(normed_ref, mixed_ref, out_ref):
    column = lax.broadcasted_iota(jnp.int32, (ENC, 1024), 1)
    row = lax.broadcasted_iota(jnp.int32, (ENC, 1024), 0)
    place = jnp.where((column % 8 < 7) & (row == column // 8 * 7 + column % 8), 1.0, 0.0).astype(bf16)
    out_ref[:, :1024] = nn(normed_ref[...], place).astype(bf16)
    out_ref[:, 1024:] = nn(mixed_ref[...], place).astype(bf16)


def spread(normed, mixed):
    return pl.pallas_call(
        spread_kernel,
        out_shape=jax.ShapeDtypeStruct((TOK, 2048), bf16),
        compiler_params=params(24),
        cost_estimate=cost(5 * 10**8, 10**6),
    )(normed, mixed)


def cross_kernel(per, slots_ref, q_ref, up_ref, weight_ref, *rest):
    sources, rest = rest[:8], rest[8:]
    out_ref, grad_ref, pairs_ref, sum_ref, far_ref, rows_ref, turned_ref, held_ref = rest

    @pl.when(pl.program_id(0) == 0)
    def _():
        for n, source in enumerate(sources):
            rows_ref[n * TOK : (n + 1) * TOK] = source[...]
            turned_ref[:, n * TOK : (n + 1) * TOK] = source[...].T

    scale = 1.0 / math.sqrt(HS)
    length = q_ref.shape[1]
    none = jnp.zeros((length, HS), bf16)
    spans = range(q_ref.shape[0])
    rows = [
        [pl.ds(pl.multiple_of(slots_ref[2 * c + n] * TOK, TOK), TOK) for n in range(2)] for c in spans
    ]
    held_ref[...] = nn(rows_ref[...], weight_ref[...]).astype(bf16)
    for first in range(0, per, 2):
        units = []
        for h in range(first, first + 2):
            at, pair = slice(h * HS, (h + 1) * HS), slice(2 * h * HS, 2 * (h + 1) * HS)
            for c in spans:
                held = jnp.concatenate([held_ref[r, pair] for r in rows[c]], axis=0)
                top = jnp.concatenate([q_ref[c, :, at], none], axis=1)
                low = jnp.concatenate([none, up_ref[c, :, at]], axis=1)
                x = jnp.concatenate([top, low], axis=0)
                units.append((c, at, pair, held, x, nt(x, held)))
        mixed = []
        for c, at, pair, held, x, s in units:
            probs = softmax(s[:length] * scale)
            grad_probs = s[length:]
            total = jnp.sum(probs * grad_probs, axis=-1, keepdims=True)
            y = jnp.concatenate([probs * (grad_probs - total), probs], axis=0).astype(bf16)
            mixed.append((c, at, pair, held, x, y))
        for c, at, pair, held, x, y in mixed:
            z = nn(y, held)
            grad_ref[c, :, at] = (z[:length, :HS] * scale).astype(bf16)
            out_ref[c, :, at] = z[length:, HS:].astype(bf16)
            g = tn(y, x)
            g = jnp.concatenate([g[:, :HS] * scale, g[:, HS:]], axis=1).astype(bf16)
            for n in range(2):
                pairs_ref[rows[c][n], pair] = g[n * TOK : (n + 1) * TOK]
    sum_ref[...] = nn(turned_ref[...], pairs_ref[...]).astype(bf16)
    far_ref[...] = nt(pairs_ref[4 * TOK :], weight_ref[...]).astype(bf16)


def cross(slots, queries, upstream, weight, sources):
    spans, length, inner = queries.shape
    rows = len(sources) * TOK
    column = pl.BlockSpec((spans, length, inner), lambda i, s: (0, 0, i))
    return pl.pallas_call(
        functools.partial(cross_kernel, inner // HS),
        grid_spec=pltpu.PrefetchScalarGridSpec(
            num_scalar_prefetch=1,
            grid=(1,),
            in_specs=[
                column,
                column,
                pl.BlockSpec((ENC, 2 * inner), lambda i, s: (0, i)),
                *[pl.BlockSpec((TOK, ENC), lambda i, s: (0, 0))] * len(sources),
            ],
            out_specs=(
                column,
                column,
                pl.BlockSpec((rows, 2 * inner), lambda i, s: (0, i)),
                pl.BlockSpec((ENC, 2 * inner), lambda i, s: (0, i)),
                pl.BlockSpec((4 * TOK, ENC), lambda i, s: (0, 0)),
            ),
            scratch_shapes=[
                pltpu.VMEM((rows, ENC), bf16),
                pltpu.VMEM((ENC, rows), bf16),
                pltpu.VMEM((rows, 2 * inner), bf16),
            ],
        ),
        out_shape=(
            jax.ShapeDtypeStruct(queries.shape, bf16),
            jax.ShapeDtypeStruct(queries.shape, bf16),
            jax.ShapeDtypeStruct((rows, 2 * inner), bf16),
            jax.ShapeDtypeStruct((ENC, 2 * inner), bf16),
            jax.ShapeDtypeStruct((4 * TOK, ENC), bf16),
        ),
        compiler_params=params(58, 1),
        cost_estimate=cost(16 * 10**9, 16 * 10**6),
    )(slots, queries, upstream, weight, *sources)


def place_kernel(sum_ref, out_ref, held_ref, made_ref, sems):
    steps = 8
    size, many = sum_ref.shape[0] // steps, sum_ref.shape[1] // HS
    ins, outs = [], []
    for i in range(steps):
        at = slice(i * size, (i + 1) * size)
        ins.append(pltpu.make_async_copy(sum_ref.at[at], held_ref.at[at], sems.at[i]))
        ins[i].start()
    for i in range(steps):
        at, to = slice(i * size, (i + 1) * size), slice(i * size * many, (i + 1) * size * many)
        ins[i].wait()
        made_ref[to] = held_ref[at].astype(f32).reshape(size, many, HS).reshape(size * many, HS)
        outs.append(pltpu.make_async_copy(made_ref.at[to], out_ref.at[to], sems.at[steps + i]))
        outs[i].start()
    for copy in outs:
        copy.wait()


def placed(summed):
    many = summed.shape[1] // HS
    hbm = pl.BlockSpec(memory_space=pltpu.HBM)
    return pl.pallas_call(
        place_kernel,
        in_specs=[hbm],
        out_specs=hbm,
        out_shape=jax.ShapeDtypeStruct((ENC * many, HS), f32),
        scratch_shapes=[
            pltpu.VMEM(summed.shape, bf16),
            pltpu.VMEM((ENC * many, HS), f32),
            pltpu.SemaphoreType.DMA((16,)),
        ],
        compiler_params=params(58),
        cost_estimate=cost(10**6, 11 * 10**6),
    )(summed)


def near_kernel(pairs_ref, weight_ref, brought_ref, *outs):
    total = nt(pairs_ref[...], weight_ref[...]) + brought_ref[...].astype(f32)
    for n, out in enumerate(outs):
        out[...] = total[n * TOK : (n + 1) * TOK].astype(bf16)


def near_sums(pairs, weight, brought):
    def whole(*shape):
        return pl.BlockSpec(shape, lambda i: (0, 0))

    inner = weight.shape[1]
    return pl.pallas_call(
        near_kernel,
        grid=(1,),
        in_specs=[whole(4 * TOK, inner), whole(ENC, inner), whole(4 * TOK, ENC)],
        out_specs=[whole(TOK, ENC)] * 4,
        out_shape=[jax.ShapeDtypeStruct((TOK, ENC), bf16)] * 4,
        compiler_params=params(32, 1),
        cost_estimate=cost(10**4, 10**4),
    )(pairs, weight, brought)


def columns_of(at):
    return at // LANES, slice(at % LANES, at % LANES + HS)


def backward_kernel(grad_ref, projected_ref, mix_ref, out_ref):
    grad = grad_ref[...]
    grad_mixed = nt(grad, mix_ref[...]).astype(bf16)
    heads = ENC // HS
    for j in range(PARTS * LANES // HS):
        part, lanes = columns_of(j * HS)
        if j < 3 * heads:
            continue
        near = j - 24
        if 0 <= near < heads:
            out_ref[part, :, lanes] = grad[:, near * HS : (near + 1) * HS]
        else:
            out_ref[part, :, lanes] = jnp.zeros((TOK, HS), bf16)
    for h in range(heads):
        q, k, v = (head(projected_ref, h, b) for b in range(3))
        g = grad_mixed[:, h * HS : (h + 1) * HS]
        probs = softmax(nt(q, k) / math.sqrt(HS))
        grad_probs = nt(g, v).astype(bf16).astype(f32)
        total = jnp.sum(probs * grad_probs, axis=-1, keepdims=True)
        grad_scores = (probs * (grad_probs - total) / math.sqrt(HS)).astype(bf16)
        for b, value in enumerate(
            (nn(grad_scores, k), tn(grad_scores, q), tn(probs.astype(bf16), g))
        ):
            part, lanes = columns_of(b * ENC + h * HS)
            out_ref[part, :, lanes] = value.astype(bf16)


def backward(grad, projected, mix):
    return pl.pallas_call(
        backward_kernel,
        out_shape=jax.ShapeDtypeStruct((PARTS, TOK, LANES), bf16),
        compiler_params=params(24),
        cost_estimate=cost(10**4, 10**4),
    )(grad, projected, mix)


def inputs_kernel(x_ref, gain_ref, project_ref, parts_ref, grad_ref, out_ref):
    many = 3 * ENC // LANES
    total = nt(parts_ref[0], project_ref[:, :LANES])
    for j in range(1, many):
        total += nt(parts_ref[j], project_ref[:, j * LANES : (j + 1) * LANES])
    rest = 3 * ENC - many * LANES
    total += nt(parts_ref[many][:, :rest], project_ref[:, many * LANES :])
    u = total.astype(bf16).astype(f32) * gain_ref[...]
    x = x_ref[...].astype(f32)
    r = lax.rsqrt(jnp.mean(x * x, axis=-1, keepdims=True) + epsilon)
    slope = jnp.mean(x * u, axis=-1, keepdims=True) * (r * r * r)
    out_ref[...] = (r * u - x * slope + grad_ref[...].astype(f32)).astype(bf16)


def inputs_grad(x, gain, project, parts, grad):
    return pl.pallas_call(
        inputs_kernel,
        out_shape=jax.ShapeDtypeStruct((TOK, ENC), bf16),
        compiler_params=params(24),
        cost_estimate=cost(10**4, 10**4),
    )(x, gain, project, parts, grad)


def shards(
    neighbour_inputs,
    encoder_gain,
    encoder_project,
    encoder_mix,
    decoder_queries,
    cross_pairs,
    span_neighbours,
    grad_output,
):
    gain = encoder_gain.reshape(1, ENC)
    y, core = lax.axis_index("y"), lax.axis_index("c")
    inner = cross_pairs.shape[2]
    inner = cross_pairs.shape[2]
    x = neighbour_inputs[0]
    heads = inner // HS
    weight = cross_pairs.reshape(ENC, 2, heads, HS).swapaxes(1, 2).reshape(ENC, 2 * inner)
    encoded, normed, projected, mixed = encode(x, gain, encoder_project, encoder_mix)

    column = [sent(encoded, step) for step in range(4)]
    column[3], weight = lax.optimization_barrier((column[3], weight))
    sources = column + [across(one) for one in column]
    operands, sources = lax.optimization_barrier((spread(normed, mixed), sources))
    operands = lax.all_gather(operands, TP, tiled=True)

    named = span_neighbours.reshape(-1) % 8
    slots = (named % 2 != core) * 4 + (named // 2 - y) % 4
    result, grad_queries, grad_pairs, grad_weight, far = cross(
        slots.astype(jnp.int32), decoder_queries, grad_output, weight, sources
    )
    summed = lax.psum(grad_weight, PLANE)

    brought = across(far)
    total = sum(
        sent_back(one, step).astype(f32)
        for step, one in enumerate(near_sums(grad_pairs, weight, brought))
    )
    grad_encoded = total.astype(bf16)

    parts = backward(grad_encoded, projected, encoder_mix)
    all_parts = lax.all_to_all(parts, TP, 0, 0, tiled=True).reshape(8 * TOK, LANES)
    mine = jnp.where(y * 2 + core < 6, operands[:, :1024], operands[:, 1024:])
    encoder_grad = nn(lax.optimization_barrier(mine.T), all_parts).astype(bf16).reshape(128, 8, LANES)
    arrived = lax.all_to_all(encoder_grad, FINE, 0, 0, tiled=True).astype(f32)
    arrived = arrived.reshape(2, 8, 8, 8, LANES).sum(axis=(0, 2))
    rows = jnp.swapaxes(arrived, 0, 1).reshape(8, 8 * LANES)[:7]
    grad_project, grad_mix = rows[:, : 3 * ENC], rows[:, 6 * LANES : 6 * LANES + ENC]
    grad_inputs = inputs_grad(x, gain, encoder_project, parts, grad_encoded)[None]
    summed, grad_project, grad_mix, grad_inputs = lax.optimization_barrier(
        (summed, grad_project, grad_mix, grad_inputs)
    )
    grad_cross = placed(summed).reshape(ENC, heads, 2, HS).swapaxes(1, 2).reshape(cross_pairs.shape)
    return result, grad_queries, grad_cross, grad_project, grad_mix, grad_inputs


def solution(mesh):
    fine = Mesh(mesh.devices.reshape(2, 4, 2, 2, 4), FINE)
    heads = P(PLANE, None, TP)
    placed = (
        P(FINE, None, None),
        P(),
        P(),
        P(),
        heads,
        P(None, None, TP),
        P(PLANE, None),
        heads,
    )
    return jax.shard_map(
        shards,
        mesh=fine,
        in_specs=placed,
        out_specs=(
            heads,
            heads,
            P(None, None, TP),
            P(FINE, None),
            P(FINE, None),
            P(FINE, None, None),
        ),
        check_vma=False,
    )
```
